32 devices in a mesh: dp: 4 (over z), ctx: 4 (over y, x), tensor: 2 (over core).
Axes of the slice: x: 2, y: 2, z: 4, core: 2. Of those that a mesh axis runs over, the one named last changes fastest.
Arguments:
- tokens: bfloat16 [32, 1024, 1024], P('dp', 'ctx'), may hold values from -6 to 6
- norm_gain: bfloat16 [1024], P(('dp', 'ctx')), may hold values from 0.5 to 1.5
- w_zx: bfloat16 [1024, 2, 2048], P(('dp', 'ctx'), None, 'tensor'), may hold values from -0.1875 to 0.1875
- w_dt: bfloat16 [1024, 32], P(('dp', 'ctx'), 'tensor'), may hold values from -0.1875 to 0.1875
- w_bc: bfloat16 [1024, 256], P(('dp', 'ctx')), may hold values from -0.1875 to 0.1875
- conv_x_w: float32 [4, 2048], P(None, 'tensor'), may hold values from -3 to 3
- conv_x_b: float32 [2048], P('tensor'), may hold values from -0.5 to 0.5
- conv_bc_w: float32 [4, 256], replicated, may hold values from -3 to 3
- conv_bc_b: float32 [256], replicated, may hold values from -0.5 to 0.5
- dt_bias: float32 [32], P('tensor'), may hold values from -4 to -1
- a_log: float32 [32], P('tensor'), may hold values from -6.9 to -0.7
- d_skip: float32 [32], P('tensor'), may hold values from 0.5 to 1.5
- norm_w: float32 [2048], P('tensor'), may hold values from 0.5 to 1.5
- w_out: bfloat16 [1024, 2048], P(('dp', 'ctx'), 'tensor'), may hold values from -0.125 to 0.125
- output_gradient: bfloat16 [32, 1024, 1024], P('dp', 'ctx'), may hold values from -6 to 6
Outputs:
- mixed_out: bfloat16 [32, 1024, 1024], P('dp', 'ctx')
- grad_tokens: float32 [32, 1024, 1024], P('dp', 'ctx')
- grad_norm_gain: float32 [1024], P(('dp', 'ctx'))
- grad_w_zx: float32 [1024, 2, 2048], P(('dp', 'ctx'), None, 'tensor')
- grad_w_dt: float32 [1024, 32], P(('dp', 'ctx'), 'tensor')
- grad_w_bc: float32 [1024, 256], P(('dp', 'ctx'))
- grad_conv_x_w: float32 [4, 2048], P(None, 'tensor')
- grad_conv_x_b: float32 [2048], P('tensor')
- grad_conv_bc_w: float32 [4, 256], replicated
- grad_conv_bc_b: float32 [256], replicated
- grad_dt_bias: float32 [32], P('tensor')
- grad_a_log: float32 [32], P('tensor')
- grad_d_skip: float32 [32], P('tensor')
- grad_norm_w: float32 [2048], P('tensor')
- grad_w_out: float32 [1024, 2048], P(('dp', 'ctx'), 'tensor')
The draws below stay inside these ranges and needn't reach their ends.
All inputs are finite; a program needn't handle non-finite values.
Results may differ from the reference program's by a relative error of at most 0.012.
The reference program's roundings to bfloat16 on the way count: a program that leaves them out, or rounds other values in their place, can miss the bound.
Values may be sent and summed in bfloat16 or wider, within the bound.
No kernel may reach another device: no remote copies, remote signals or barrier semaphores. Data moves between devices by JAX's collectives and lax.ppermute only.
A program may use at most 256 MiB of HBM per device.

```python
import jax
import jax.numpy as jnp
from jax import lax

D = 1024
HEADS = 32
P_SIZE = 64
N = 128
K = 4
SPAN = 256
SEQ_LEN = 1024
INNER = 2048
SEQS = 32
N_TENSOR = 2


def block_scale(own_key, shape, cuts, smallest, largest):
    gain = 1.0
    for dim, blocks in cuts:
        heights = jax.random.uniform(jax.random.fold_in(jax.random.fold_in(own_key, 6), dim), (blocks,), jnp.float32, smallest / len(cuts), largest / len(cuts))
        gain = gain * jnp.repeat(jnp.exp(heights), shape[dim] // blocks).reshape((-1,) + (1,) * (len(shape) - 1 - dim))
    return gain


def scatter_about(rng, shape, scale, reach, cuts=(), kind=jnp.bfloat16):
    entries = jax.random.normal(rng, shape, jnp.float32) * scale
    if len(cuts) > 0:
        entries = block_scale(rng, shape, cuts, -0.22, 0.18) * entries
    return jnp.clip(entries, min=-reach, max=reach).astype(kind)


def setup_inputs(seed: int = 0) -> dict:
    splits = jax.random.split(jax.random.key(seed), 16)
    tokens = scatter_about(splits[0], (SEQS, SEQ_LEN, D), 1.0, 6.0, ((0, 4), (1, 4)))
    norm_gain = jnp.clip(1.0 + 0.1 * jax.random.normal(splits[1], (D,), jnp.float32), 0.5, 1.5).astype(jnp.bfloat16)
    w_zx = scatter_about(splits[2], (D, 2, INNER), D ** -0.5, 0.1875, ((0, 16), (2, 2)))
    w_dt = scatter_about(splits[3], (D, HEADS), D ** -0.5, 0.1875, ((0, 16), (1, 2)))
    w_bc = scatter_about(splits[4], (D, 2 * N), D ** -0.5, 0.1875, ((0, 16),))
    conv_x_w = scatter_about(splits[5], (K, INNER), K ** -0.5, 3.0, ((1, 2),), jnp.float32)
    conv_x_b = jnp.clip(jax.random.uniform(splits[6], (INNER,), jnp.float32, -0.5, 0.5) * block_scale(splits[6], (INNER,), ((0, 2),), -0.4, 0.0), -0.5, 0.5)
    conv_bc_w = scatter_about(splits[7], (K, 2 * N), K ** -0.5, 3.0, (), jnp.float32)
    conv_bc_b = jnp.clip(jax.random.uniform(splits[8], (2 * N,), jnp.float32, -0.5, 0.5), -0.5, 0.5)
    dt_bias = jnp.clip(-4.0 + 3.0 * jax.random.uniform(splits[9], (HEADS,), jnp.float32) ** block_scale(splits[9], (HEADS,), ((0, 2),), -0.2, 0.2), -4.0, -1.0)
    a_log = jnp.clip(-6.9 + 6.2000001 * jax.random.uniform(splits[10], (HEADS,), jnp.float32) ** block_scale(splits[10], (HEADS,), ((0, 2),), -0.2, 0.2), -6.9, -0.7)
    d_skip = jnp.clip(0.5 + 1.0 * jax.random.uniform(splits[11], (HEADS,), jnp.float32) ** block_scale(splits[11], (HEADS,), ((0, 2),), -0.2, 0.2), 0.5, 1.5)
    norm_w = jnp.clip(1.0 + 0.1 * jax.random.normal(splits[12], (INNER,), jnp.float32), 0.5, 1.5)
    w_out = scatter_about(splits[13], (D, INNER), INNER ** -0.5, 0.125, ((0, 16), (1, 2)))
    output_gradient = scatter_about(splits[14], (SEQS, SEQ_LEN, D), 1.0, 6.0, ((0, 4), (1, 4)))
    return dict(tokens=tokens, norm_gain=norm_gain, w_zx=w_zx, w_dt=w_dt, w_bc=w_bc, conv_x_w=conv_x_w, conv_x_b=conv_x_b, conv_bc_w=conv_bc_w, conv_bc_b=conv_bc_b, dt_bias=dt_bias, a_log=a_log, d_skip=d_skip, norm_w=norm_w, w_out=w_out, output_gradient=output_gradient)


EPS = 1e-05
HIGH = lax.Precision.HIGHEST

@jax.custom_vjp
def low(v):
    return lax.optimization_barrier(v.astype(jnp.bfloat16)).astype(jnp.float32)

@jax.custom_vjp
def low_back(v):
    return v

def low_keep(v):
    return (low(v), None)

def low_pass(kept, grad):
    return (grad,)

def back_keep(v):
    return (v, None)

def back_low(kept, grad):
    return (low(grad),)
low.defvjp(low_keep, low_pass)
low_back.defvjp(back_keep, back_low)

def block_step(memory, inputs, a_decay):
    values, step_size, input_map, output_map = inputs
    length = values.shape[0]
    decay_sum = jnp.cumsum(step_size * a_decay[None, :], axis=0)
    positions = jnp.arange(length)
    causal = (positions[:, None] >= positions[None, :])[:, :, None]
    spread = jnp.where(causal, decay_sum[:, None, :] - decay_sum[None, :, :], -jnp.inf)
    scores = jnp.dot(output_map, input_map.T, precision=HIGH)
    weights = jnp.exp(spread) * scores[:, :, None]
    scaled = values * step_size[:, :, None]
    inside = jnp.einsum('tsh,shp->thp', weights, scaled, precision=HIGH)
    from_memory = jnp.exp(decay_sum)[:, :, None] * jnp.einsum('hpn,tn->thp', memory, output_map, precision=HIGH)
    closing = decay_sum[-1]
    remaining = jnp.exp(closing[None, :] - decay_sum)
    new_memory = jnp.exp(closing)[:, None, None] * memory + jnp.einsum('shp,sn->hpn', remaining[:, :, None] * scaled, input_map, precision=HIGH)
    return (new_memory, inside + from_memory)

def ssd_sequence(values, step_size, a_decay, input_map, output_map):
    blocks = values.shape[0] // SPAN

    def advance(memory, inputs):
        return jax.checkpoint(block_step)(memory, inputs, a_decay)

    def blocked(stacked):
        return stacked.reshape((blocks, SPAN) + stacked.shape[1:])
    initial = jnp.zeros((values.shape[1], values.shape[2], input_map.shape[1]), jnp.float32)
    final_memory, outputs = lax.scan(advance, initial, (blocked(values), blocked(step_size), blocked(input_map), blocked(output_map)))
    return outputs.reshape(values.shape)

def causal_conv(sequence, weight, bias):
    conv_taps = weight.shape[0]
    length = sequence.shape[0]
    padded = jnp.concatenate([jnp.zeros((conv_taps - 1, sequence.shape[1]), jnp.float32), sequence], 0)
    return bias[None, :] + sum((padded[offset:offset + length] * weight[offset][None, :] for offset in range(conv_taps)))

def layer(sequence, norm_gain, w_zx, w_dt, w_bc, conv_x_w, conv_x_b, conv_bc_w, conv_bc_b, dt_bias, a_log, d_skip, norm_w, w_out):
    length = sequence.shape[0]
    normalized_rows = sequence * lax.rsqrt(lax.optimization_barrier(jnp.mean(sequence * sequence, axis=-1, keepdims=True)) + EPS) * norm_gain
    normalized_rows = low(normalized_rows)
    projected_rows = jnp.einsum('ld,dki->lki', normalized_rows, w_zx, precision=HIGH)
    gate_raw = low_back(projected_rows[:, 0])
    inner_raw = low(low_back(projected_rows[:, 1]))
    unmixed_timestep = low_back(jnp.dot(normalized_rows, w_dt, precision=HIGH))
    unmixed_bc_values = jnp.dot(normalized_rows, w_bc, precision=HIGH)
    values = jax.nn.silu(causal_conv(inner_raw, conv_x_w, conv_x_b)).reshape(length, HEADS, P_SIZE)
    step_size = jax.nn.softplus(unmixed_timestep + dt_bias)
    a_decay = -jnp.exp(a_log)
    group_heads = HEADS // N_TENSOR
    pieces = []
    for member in range(N_TENSOR):
        bc_group = low(low_back(unmixed_bc_values))
        bc_conv = jax.nn.silu(causal_conv(bc_group, conv_bc_w, conv_bc_b))
        heads_part = slice(member * group_heads, (member + 1) * group_heads)
        pieces.append(ssd_sequence(values[:, heads_part], step_size[:, heads_part], a_decay[heads_part], bc_conv[:, :N], bc_conv[:, N:]))
    y_ssd = jnp.concatenate(pieces, 1) + d_skip[None, :, None] * values
    gated_rows = y_ssd.reshape(length, INNER) * jax.nn.silu(gate_raw)
    inv_rms = lax.rsqrt(lax.optimization_barrier(jnp.mean(gated_rows * gated_rows, axis=-1, keepdims=True)) + EPS)
    mixer_input_rows = low(gated_rows * inv_rms * norm_w)
    return sequence + jnp.dot(mixer_input_rows, w_out.T, precision=HIGH)

def reference(tokens, norm_gain, w_zx, w_dt, w_bc, conv_x_w, conv_x_b, conv_bc_w, conv_bc_b, dt_bias, a_log, d_skip, norm_w, w_out, output_gradient):
    weights = (norm_gain.astype(jnp.float32), w_zx.astype(jnp.float32), w_dt.astype(jnp.float32), w_bc.astype(jnp.float32), conv_x_w, conv_x_b, conv_bc_w, conv_bc_b, dt_bias, a_log, d_skip, norm_w, w_out.astype(jnp.float32))
    inputs = tokens.astype(jnp.float32)
    cotangent = output_gradient.astype(jnp.float32)

    def one_sequence(totals, pair):
        sequence, seq_cot = pair
        result, pullback = jax.vjp(layer, sequence, *weights)
        grads = pullback(seq_cot)
        summed = tuple((total + grad for total, grad in zip(totals, grads[1:])))
        return (summed, (result.astype(jnp.bfloat16), grads[0]))
    initial = tuple((jnp.zeros_like(weight) for weight in weights))
    sums, (outputs, input_grads) = lax.scan(one_sequence, initial, (inputs, cotangent))
    return (outputs, input_grads, sums[0], sums[1], sums[2], sums[3], sums[4], sums[5], sums[6], sums[7], sums[8], sums[9], sums[10], sums[11], sums[12])
```

```python
from functools import partial

import jax
import jax.numpy as jnp
from jax import lax
from jax.experimental import pallas as pl
from jax.experimental.pallas import tpu as pltpu
from jax.sharding import PartitionSpec as P

EPS = 1e-05
LOG2E = 1.4426950408889634
LANES = 128
HIGH = lax.Precision.HIGHEST
BF = jnp.bfloat16
F32 = jnp.float32


def bits_of(axis):
    return [1 << i for i in reversed(range(lax.axis_size(axis).bit_length() - 1))]


def swap(block, axis, mask):
    return lax.ppermute(block, axis, [(i, i ^ mask) for i in range(lax.axis_size(axis))])


def side(axis, bit):
    return (lax.axis_index(axis) // bit) % 2


def row_bits():
    return [("dp", b) for b in bits_of("dp")] + [("ctx", b) for b in bits_of("ctx")]


def gather_rows(shard, order):
    places = row_bits()
    whole = shard.reshape((1,) * len(places) + shard.shape)
    for place in order:
        dim = places.index(place)
        other = swap(whole, *place)
        whole = jnp.where(
            side(*place) == 1,
            jnp.concatenate([other, whole], dim),
            jnp.concatenate([whole, other], dim),
        )
    return whole.reshape((-1,) + shard.shape[1:])


def halve(part, dim, place):
    up = side(*place)
    mine = lax.dynamic_index_in_dim(part, up, dim)
    theirs = lax.dynamic_index_in_dim(part, 1 - up, dim)
    return mine + swap(theirs.astype(BF), *place).astype(F32)


def scatter_rows(part, order):
    places = row_bits()
    left = part.reshape((2,) * len(places) + (part.shape[0] >> len(places),) + part.shape[1:])
    for place in order:
        left = halve(left, places.index(place), place)
    return left.reshape(left.shape[len(places) :])


def sum_over(part, places):
    for place in places:
        part = part + swap(part, *place)
    return part


def spread_out(blocks, length):
    parts = lax.axis_size("ctx")
    me = lax.axis_index("ctx")
    cuts = lax.axis_size("tensor")
    rows = length // cuts
    width = blocks.shape[-1]
    seqs = blocks.shape[0] // parts
    mine = lax.dynamic_slice_in_dim(blocks, lax.axis_index("tensor") * rows, rows, 1)
    mine = mine.reshape(parts, seqs, rows, width)
    slots = []
    for k in range(parts):
        piece = lax.dynamic_index_in_dim(mine, me ^ k, 0, False)
        slots.append(swap(piece, "ctx", k) if k else piece)
    return gather_cuts(jnp.stack(slots))


def gather_cuts(share):
    for bit in reversed(bits_of("tensor")):
        other = swap(share, "tensor", bit)
        share = jnp.where(
            side("tensor", bit) == 1,
            jnp.concatenate([other, share], 2),
            jnp.concatenate([share, other], 2),
        )
    return share


def cut_sum(part):
    bits = bits_of("tensor")
    slots, seqs, length, width = part.shape
    left = part.reshape((slots, seqs) + (2,) * len(bits) + (length >> len(bits), width))
    for dim, bit in enumerate(bits):
        left = halve(left, 2 + dim, ("tensor", bit))
    return left.reshape(slots, seqs, -1, width)


def send_home(share):
    parts = lax.axis_size("ctx")
    me = lax.axis_index("ctx")
    home = jnp.stack([swap(share[k], "ctx", k) if k else share[k] for k in range(parts)])
    home = gather_cuts(home)
    home = jnp.concatenate([lax.dynamic_index_in_dim(home, me ^ k, 0) for k in range(parts)])
    return home.reshape((-1,) + home.shape[2:])


def dot(a, b, dims):
    return lax.dot_general(a, b, (dims, ((), ())), preferred_element_type=F32)


NN = ((1,), (0,))
NT = ((1,), (1,))
TN = ((0,), (0,))


def tiled(lanes, width):
    return jnp.concatenate([lanes] * (width // lanes.shape[1]), 1)


def conv_rows(raw, before, weight):
    taps = len(weight) - 1
    width = raw.shape[1]
    ext = jnp.concatenate([before, raw], 1)
    total = tiled(weight[taps], width) + tiled(weight[taps - 1], width) * raw
    for k in range(1, taps):
        total += tiled(weight[taps - 1 - k], width) * pltpu.roll(ext, k, 1)[:, LANES:]
    return total


def fold(rows):
    return sum(rows[:, i : i + LANES] for i in range(0, rows.shape[1], LANES))


def conv_back(grad, after, raw, weight, totals):
    taps = len(weight) - 1
    width = grad.shape[1]
    ext = jnp.concatenate([grad, after], 1)
    out = tiled(weight[taps - 1], width) * grad
    totals[taps][...] += fold(grad)
    totals[taps - 1][...] += fold(grad * raw)
    for k in range(1, taps):
        moved = pltpu.roll(ext, width + LANES - k, 1)[:, :width]
        out += tiled(weight[taps - 1 - k], width) * moved
        totals[taps - 1 - k][...] += fold(moved * raw)
    return out


def order_mask(width, keep):
    row = lax.broadcasted_iota(jnp.int32, (width, width), 0)
    col = lax.broadcasted_iota(jnp.int32, (width, width), 1)
    return keep(row, col)


def head_rows(dt_raw, dt_bias, a_log):
    biased = dt_raw + dt_bias
    step = jnp.maximum(biased, 0.0) + jnp.log1p(jnp.exp(-jnp.abs(biased)))
    a_decay = -jnp.exp(a_log)
    return biased, step, a_decay


def fill_heads(cs, heads, cs_ref, col_ref, ecs_ref, rem_ref, end_ref):
    width = cs.shape[1]
    cs2 = cs * LOG2E
    cs_ref[...] = cs2
    last = jnp.broadcast_to(cs2[:, width - 1 :], cs2.shape)
    ecs_ref[...] = jnp.exp2(cs2)
    rem_ref[...] = jnp.exp2(last - cs2)
    end_ref[...] = jnp.exp2(last[:, :LANES])
    columns = jnp.transpose(cs2)
    for h in range(heads):
        col_ref[h] = jnp.broadcast_to(columns[:, h : h + 1], (width, LANES))


def decay_blocks(cs_row, column):
    count = cs_row.shape[1] // LANES
    out = {}
    for i in range(count):
        for j in range(i, count):
            gap = cs_row[:, j * LANES : (j + 1) * LANES] - column[i * LANES : (i + 1) * LANES]
            out[i, j] = jnp.exp2(jnp.minimum(gap, 0.0) if i == j else gap)
    return out


def block(ref, i, j):
    return ref[i * LANES : (i + 1) * LANES, j * LANES : (j + 1) * LANES]


def mixing(decay, score_ref):
    count = score_ref.shape[0] // LANES
    none = jnp.zeros((LANES, LANES), BF)
    return jnp.concatenate(
        [
            jnp.concatenate(
                [
                    (decay[i, j] * block(score_ref, i, j)).astype(BF) if j >= i else none
                    for j in range(count)
                ],
                1,
            )
            for i in range(count)
        ],
        0,
    )


def forward_kernel(
    heads, me, raw, bc_raw, dt_raw, cw, cbw, hp,
    z_out, zbc_out, y_out, cs_out, mem_out,
    mem, before, before_bc, step_s, cs_s, col_s, ecs_s, rem_s, end_s, score_s, maps_s,
):
    head_size = raw.shape[2] // heads
    half = bc_raw.shape[2] // 2
    width = raw.shape[3]
    taps = cw.shape[0]

    @pl.when(pl.program_id(1) == 0)
    def _():
        mem[...] = jnp.zeros_like(mem)
        before[...] = jnp.zeros_like(before)
        before_bc[...] = jnp.zeros_like(before_bc)

    bc = bc_raw[0, 0].astype(F32)
    zbc = conv_rows(bc, before_bc[...], [cbw[j] for j in range(taps)])
    before_bc[...] = bc[:, width - LANES :]
    zbc_out[0, 0] = zbc
    maps_s[...] = (zbc * jax.nn.sigmoid(zbc)).astype(BF)
    causal = order_mask(width, lambda s, t: s <= t)
    score_s[...] = jnp.where(causal, dot(maps_s[:half], maps_s[half:], TN), 0.0)

    _, step, a_decay = head_rows(dt_raw[0, 0], hp[0], hp[1])
    cs = jnp.dot(step * a_decay, causal.astype(F32), precision=HIGH, preferred_element_type=F32)
    cs_out[0, 0] = cs
    step_s[...] = step
    fill_heads(cs, heads, cs_s, col_s, ecs_s, rem_s, end_s)

    def one(h, carry):
        rows = pl.ds(pl.multiple_of(h * head_size, head_size), head_size)
        row = pl.ds(h, 1)
        own = raw[0, 0, rows, :].astype(F32)
        z = conv_rows(own, before[rows, :], [cw[j, rows, :] for j in range(taps)])
        before[rows, :] = own[:, width - LANES :]
        z_out[0, 0, rows, :] = z
        x = z * jax.nn.sigmoid(z)
        scaled = x * step_s[row, :]
        decay = decay_blocks(cs_s[row, :], col_s[h])
        inside = dot(scaled.astype(BF), mixing(decay, score_s), NN)
        memory = mem[rows, :]
        memory_low = memory.astype(BF)
        mem_out[0, 0, rows, :] = memory_low
        held = dot(memory_low, maps_s[half:], NN) * ecs_s[row, :]
        y_out[0, 0, rows, :] = inside + held + hp[2, row, :] * x
        gained = dot((scaled * rem_s[row, :]).astype(BF), maps_s[:half], NT)
        mem[rows, :] = memory * end_s[row, :] + gained
        return carry

    lax.fori_loop(0, heads, one, 0)


def backward_kernel(
    heads, me, z_in, raw, y_in, g_in, zbc_in, bc_raw, dt_raw, cs_in, mem_in, cw, cbw, hp,
    gin_out, gbc_out, gdt_out, sum_x, sum_bc, sum_h,
    gmem, gmem_low, after, after_bc, step_s, cs_s, col_s, ecs_s, rem_s, end_s, score_s, maps_s,
    gscore_s, eg_s, rx_s, pq_s, e_s, r_s, d_s, k_s,
):
    head_size = raw.shape[2] // heads
    half = bc_raw.shape[2] // 2
    width = raw.shape[3]
    taps = cw.shape[0]
    count = width // LANES

    @pl.when((pl.program_id(0) == 0) & (pl.program_id(1) == 0))
    def _():
        sum_x[...] = jnp.zeros_like(sum_x)
        sum_bc[...] = jnp.zeros_like(sum_bc)
        sum_h[...] = jnp.zeros_like(sum_h)
        pq_s[...] = jnp.zeros_like(pq_s)
        e_s[...] = jnp.zeros_like(e_s)
        r_s[...] = jnp.zeros_like(r_s)
        d_s[...] = jnp.zeros_like(d_s)
        k_s[...] = jnp.zeros_like(k_s)

    @pl.when(pl.program_id(1) == 0)
    def _():
        gmem[...] = jnp.zeros_like(gmem)
        after[...] = jnp.zeros_like(after)
        after_bc[...] = jnp.zeros_like(after_bc)

    zbc = zbc_in[0, 0]
    sig_bc = jax.nn.sigmoid(zbc)
    maps_s[...] = (zbc * sig_bc).astype(BF)
    causal = order_mask(width, lambda s, t: s <= t)
    score_s[...] = jnp.where(causal, dot(maps_s[:half], maps_s[half:], TN), 0.0)
    gscore_s[...] = jnp.zeros_like(gscore_s)

    biased, step, a_decay = head_rows(dt_raw[0, 0], hp[0], hp[1])
    step_s[...] = step
    fill_heads(cs_in[0, 0], heads, cs_s, col_s, ecs_s, rem_s, end_s)

    def one(h, carry):
        rows = pl.ds(pl.multiple_of(h * head_size, head_size), head_size)
        row = pl.ds(h, 1)
        z = z_in[0, 0, rows, :]
        sig = jax.nn.sigmoid(z)
        x = z * sig
        step_row = step_s[row, :]
        skip = hp[2, row, :]
        scaled = x * step_row
        scaled_low = scaled.astype(BF)
        scaled_back = scaled_low.astype(F32)
        g_low = g_in[0, 0, rows, :]
        g = g_low.astype(F32)
        decay = decay_blocks(cs_s[row, :], col_s[h])
        inside = dot(g_low, mixing(decay, score_s), NT)
        gweights = dot(scaled_low, g_low, TN)
        for (i, j), weight in decay.items():
            place = (slice(i * LANES, (i + 1) * LANES), slice(j * LANES, (j + 1) * LANES))
            gscore_s[place] += weight * gweights[place]
        later = gmem[rows, :]
        later_low = later.astype(BF)
        gmem_low[rows, :] = later_low
        outside = dot(later_low, maps_s[:half], NN) * rem_s[row, :]
        gscaled = inside + outside
        both = g * (y_in[0, 0, rows, :] - skip * x) - scaled_back * inside
        pq_s[row, :] = jnp.sum(both, 0, keepdims=True)
        e_s[row, :] = jnp.sum(scaled_back * outside, 0, keepdims=True)
        r_s[row, :] = jnp.sum(x * gscaled, 0, keepdims=True)
        d_s[row, :] += jnp.sum(g * x, 0, keepdims=True)
        k_s[row, :] = jnp.sum(later * mem_in[0, 0, rows, :].astype(F32), 0, keepdims=True)
        eg = (g * ecs_s[row, :]).astype(BF)
        eg_s[rows, :] = eg
        rx_s[rows, :] = (scaled * rem_s[row, :]).astype(BF)
        gmem[rows, :] = later * end_s[row, :] + dot(eg, maps_s[half:], NT)
        gz = (step_row * gscaled + skip * g) * (sig * (1.0 + z * (1.0 - sig)))
        own = raw[0, 0, rows, :].astype(F32)
        grad = conv_back(
            gz, after[rows, :], own, [cw[j, rows, :] for j in range(taps)],
            [sum_x.at[j, rows, :] for j in range(taps)],
        )
        after[rows, :] = gz[:, :LANES]
        gin_out[0, 0, rows, :] = grad.astype(BF)
        return carry

    lax.fori_loop(0, heads, one, 0)

    gscore = jnp.where(causal, gscore_s[...], 0.0).astype(BF)
    gout_map = dot(maps_s[:half], gscore, NN) + dot(mem_in[0, 0], eg_s[...], TN)
    gin_map = dot(maps_s[half:], gscore, NT) + dot(gmem_low[...], rx_s[...], TN)
    gmaps = jnp.concatenate([gin_map, gout_map], 0) * (sig_bc * (1.0 + zbc * (1.0 - sig_bc)))
    gbc = conv_back(
        gmaps, after_bc[...], bc_raw[0, 0].astype(F32), [cbw[j] for j in range(taps)],
        [sum_bc.at[j] for j in range(taps)],
    )
    after_bc[...] = gmaps[:, :LANES]
    gbc_out[0, 0] = gbc.astype(BF)

    from_here = order_mask(width, lambda t, u: t >= u).astype(F32)
    strictly = order_mask(width, lambda s, u: s < u).astype(F32)
    carried = jnp.sum(k_s[...], 1, keepdims=True) * end_s[:, :1]
    gdecay = (
        jnp.dot(pq_s[...], from_here, precision=HIGH, preferred_element_type=F32)
        + jnp.dot(e_s[...], strictly, precision=HIGH, preferred_element_type=F32)
        + carried
    )
    gdt = (a_decay * gdecay + r_s[...]) * jax.nn.sigmoid(biased)
    gdt_out[0, 0] = gdt
    sum_h[0] += fold(gdt)
    sum_h[1] += fold(gdecay * step * a_decay)

    @pl.when((pl.program_id(0) == pl.num_programs(0) - 1) & (pl.program_id(1) == pl.num_programs(1) - 1))
    def _():
        sum_h[2] = fold(d_s[...])


def run_forward(inner, bc, dt, cw, cbw, hp, heads):
    parts, seqs, rows, width = inner.shape
    maps, head_pad, states = bc.shape[2], dt.shape[2], bc.shape[2] // 2

    def part(count, last=width):
        return pl.BlockSpec((1, 1, count, last), lambda s, c, me: (c ^ me[0], s, 0, 0))

    def fixed(shape):
        return pl.BlockSpec(shape, lambda s, c, me: (0,) * len(shape))

    def shape(count, last=width, kind=F32):
        return jax.ShapeDtypeStruct((parts, seqs, count, last), kind)

    return pl.pallas_call(
        partial(forward_kernel, heads),
        grid_spec=pltpu.PrefetchScalarGridSpec(
            num_scalar_prefetch=1,
            grid=(seqs, parts),
            in_specs=[part(rows), part(maps), part(head_pad), fixed(cw.shape), fixed(cbw.shape), fixed(hp.shape)],
            out_specs=[part(rows), part(maps), part(rows), part(head_pad), part(rows, states)],
            scratch_shapes=[
                pltpu.VMEM((rows, states), F32),
                pltpu.VMEM((rows, LANES), F32),
                pltpu.VMEM((maps, LANES), F32),
                pltpu.VMEM((head_pad, width), F32),
                pltpu.VMEM((head_pad, width), F32),
                pltpu.VMEM((heads, width, LANES), F32),
                pltpu.VMEM((head_pad, width), F32),
                pltpu.VMEM((head_pad, width), F32),
                pltpu.VMEM((head_pad, LANES), F32),
                pltpu.VMEM((width, width), F32),
                pltpu.VMEM((maps, width), BF),
            ],
        ),
        out_shape=[
            shape(rows),
            shape(maps),
            shape(rows),
            shape(head_pad),
            shape(rows, states, BF),
        ],
        compiler_params=pltpu.CompilerParams(
            dimension_semantics=("arbitrary", "arbitrary"), vmem_limit_bytes=48 << 20
        ),
        cost_estimate=pl.CostEstimate(flops=4 << 30, bytes_accessed=32 << 20, transcendentals=0),
        name="scan_forward",
    )(lax.axis_index("ctx").reshape(1), inner, bc, dt, cw, cbw, hp)


def run_backward(z, inner, y, g, zbc, bc, dt, cs, mem, cw, cbw, hp, heads):
    parts, seqs, rows, width = inner.shape
    maps, head_pad, states = bc.shape[2], dt.shape[2], bc.shape[2] // 2

    def part(count, last=width):
        return pl.BlockSpec(
            (1, 1, count, last), lambda s, c, me: ((parts - 1 - c) ^ me[0], s, 0, 0)
        )

    def fixed(shape):
        return pl.BlockSpec(shape, lambda s, c, me: (0,) * len(shape))

    def shape(count, kind=F32):
        return jax.ShapeDtypeStruct((parts, seqs, count, width), kind)

    return pl.pallas_call(
        partial(backward_kernel, heads),
        grid_spec=pltpu.PrefetchScalarGridSpec(
            num_scalar_prefetch=1,
            grid=(seqs, parts),
            in_specs=[
                part(rows), part(rows), part(rows), part(rows), part(maps), part(maps),
                part(head_pad), part(head_pad), part(rows, states),
                fixed(cw.shape), fixed(cbw.shape), fixed(hp.shape),
            ],
            out_specs=[
                part(rows), part(maps), part(head_pad),
                fixed(cw.shape), fixed(cbw.shape), fixed((3, head_pad, LANES)),
            ],
            scratch_shapes=[
                pltpu.VMEM((rows, states), F32),
                pltpu.VMEM((rows, states), BF),
                pltpu.VMEM((rows, LANES), F32),
                pltpu.VMEM((maps, LANES), F32),
                pltpu.VMEM((head_pad, width), F32),
                pltpu.VMEM((head_pad, width), F32),
                pltpu.VMEM((heads, width, LANES), F32),
                pltpu.VMEM((head_pad, width), F32),
                pltpu.VMEM((head_pad, width), F32),
                pltpu.VMEM((head_pad, LANES), F32),
                pltpu.VMEM((width, width), F32),
                pltpu.VMEM((maps, width), BF),
                pltpu.VMEM((width, width), F32),
                pltpu.VMEM((rows, width), BF),
                pltpu.VMEM((rows, width), BF),
                pltpu.VMEM((head_pad, width), F32),
                pltpu.VMEM((head_pad, width), F32),
                pltpu.VMEM((head_pad, width), F32),
                pltpu.VMEM((head_pad, width), F32),
                pltpu.VMEM((head_pad, LANES), F32),
            ],
        ),
        out_shape=[
            shape(rows, BF),
            shape(maps, BF),
            shape(head_pad),
            jax.ShapeDtypeStruct(cw.shape, F32),
            jax.ShapeDtypeStruct(cbw.shape, F32),
            jax.ShapeDtypeStruct((3, head_pad, LANES), F32),
        ],
        compiler_params=pltpu.CompilerParams(
            dimension_semantics=("arbitrary", "arbitrary"), vmem_limit_bytes=48 << 20
        ),
        cost_estimate=pl.CostEstimate(flops=8 << 30, bytes_accessed=48 << 20, transcendentals=0),
        name="scan_backward",
    )(lax.axis_index("ctx").reshape(1), z, inner, y, g, zbc, bc, dt, cs, mem, cw, cbw, hp)


def project(rows, weight):
    return jnp.einsum("ksld,di->ksil", rows, weight, preferred_element_type=F32)


def project_back(grad, weight):
    return jnp.einsum("ksil,di->ksld", grad, weight, preferred_element_type=F32)


def weight_grad(rows, grad):
    return jnp.einsum("ksld,ksil->di", rows, grad, preferred_element_type=F32)


def per_device(
    tokens, norm_gain, w_zx, w_dt, w_bc, conv_x_w, conv_x_b, conv_bc_w, conv_bc_b,
    dt_bias, a_log, d_skip, norm_w, w_out, output_gradient,
):
    seqs_here, length, width = tokens.shape
    heads = w_dt.shape[1]
    head_pad = -(-heads // 8) * 8
    inner_here = w_out.shape[1]
    inner_total = inner_here * lax.axis_size("tensor")
    maps = w_bc.shape[1]
    dp_bits = [("dp", b) for b in bits_of("dp")]
    ctx_bits = [("ctx", b) for b in bits_of("ctx")]
    tensor_bits = [("tensor", b) for b in bits_of("tensor")]

    small = jnp.concatenate(
        [
            w_bc,
            jnp.pad(w_dt, ((0, 0), (0, head_pad - heads))),
            norm_gain[:, None],
            jnp.zeros((w_bc.shape[0], LANES - head_pad - 1), BF),
        ],
        1,
    )
    small = gather_rows(small, dp_bits + ctx_bits)
    full_bc = small[:, :maps]
    full_dt = small[:, maps : maps + head_pad]
    gain = small[:, maps + head_pad].astype(F32)
    full_inner = gather_rows(w_zx[:, 1], dp_bits + ctx_bits)
    rows = spread_out(tokens, length)
    full_out = gather_rows(w_out, dp_bits + ctx_bits[::-1])
    cots = spread_out(output_gradient, length)
    full_gate = gather_rows(w_zx[:, 0], dp_bits + ctx_bits)

    residual = rows.astype(F32)
    normed = (
        residual * lax.rsqrt(jnp.mean(residual * residual, axis=-1, keepdims=True) + EPS) * gain
    ).astype(BF)
    bc_raw = project(normed, full_bc).astype(BF)
    dt_raw = project(normed, full_dt)
    inner_raw = project(normed, full_inner).astype(BF)

    def lanes(column):
        return jnp.broadcast_to(column[..., None], column.shape + (LANES,))

    cw = lanes(jnp.concatenate([conv_x_w, conv_x_b[None]], 0))
    cbw = lanes(jnp.concatenate([conv_bc_w, conv_bc_b[None]], 0))
    hp = jnp.pad(jnp.stack([dt_bias, a_log, d_skip]), ((0, 0), (0, head_pad - heads)))
    hp = jnp.broadcast_to(hp[..., None], hp.shape + (length,))

    z, zbc, y, cs, mem = run_forward(inner_raw, bc_raw, dt_raw, cw, cbw, hp, heads)

    gate_raw = project(normed, full_gate)
    grad_mixed = project(cots, full_out)
    gate_sig = jax.nn.sigmoid(gate_raw)
    gate_act = gate_raw * gate_sig
    gated = y * gate_act
    norm_column = norm_w[:, None]
    weighted = grad_mixed * norm_column
    sums = jnp.stack([jnp.sum(gated * gated, axis=2), jnp.sum(weighted * gated, axis=2)])
    sums = sum_over(sums, tensor_bits)[:, :, :, None]
    inv_rms = lax.rsqrt(sums[0] / inner_total + EPS)
    mixed_in = (gated * inv_rms * norm_column).astype(BF)
    grad_norm_w = jnp.sum(grad_mixed * gated * inv_rms, axis=(0, 1, 3))
    grad_gated = inv_rms * weighted - gated * (inv_rms * inv_rms * inv_rms) * (
        sums[1] / inner_total
    )
    grad_gate = (grad_gated * y * gate_sig * (1.0 + gate_raw * (1.0 - gate_sig))).astype(BF)
    grad_y = (grad_gated * gate_act).astype(BF)

    grad_inner, grad_bc, grad_dt, sum_x, sum_bc, sum_h = run_backward(
        z, inner_raw, y, grad_y, zbc, bc_raw, dt_raw, cs, mem, cw, cbw, hp, heads
    )

    grad_w_out = scatter_rows(weight_grad(cots, mixed_in), ctx_bits + dp_bits[::-1])
    mixed = cut_sum(project_back(mixed_in, full_out))
    cuts = lax.axis_size("tensor")
    share = lax.dynamic_slice_in_dim(
        rows, lax.axis_index("tensor") * (length // cuts), length // cuts, 2
    )
    mixed_out = send_home((share.astype(F32) + mixed).astype(BF))
    grad_w_gate = scatter_rows(weight_grad(normed, grad_gate), ctx_bits[::-1] + dp_bits[::-1])

    grad_dt_low = grad_dt.astype(BF)
    grad_normed = (
        project_back(grad_gate, full_gate)
        + project_back(grad_inner, full_inner)
        + project_back(grad_dt_low, full_dt)
        + project_back(grad_bc, full_bc)
    )
    grad_home = send_home(cut_sum(grad_normed).astype(BF)).astype(F32)

    grad_w_inner = scatter_rows(weight_grad(normed, grad_inner), ctx_bits + dp_bits[::-1])
    grad_small = jnp.concatenate(
        [weight_grad(normed, grad_bc), weight_grad(normed, grad_dt_low)[:, :heads]], 1
    )
    grad_small = scatter_rows(grad_small, ctx_bits[::-1] + dp_bits[::-1])
    grad_w_bc = sum_over(grad_small[:, :maps], tensor_bits)
    grad_w_dt = grad_small[:, maps:]

    here = tokens.astype(F32)
    r = lax.rsqrt(jnp.mean(here * here, axis=-1, keepdims=True) + EPS)
    scaled = gain * grad_home
    grad_tokens = (
        output_gradient.astype(F32)
        + r * scaled
        - here * (r * r * r) * jnp.mean(here * scaled, axis=-1, keepdims=True)
    )
    grad_gain = jnp.sum(here * r * grad_home, axis=(0, 1))

    sum_x = jnp.sum(sum_x, -1)
    sum_bc = jnp.sum(sum_bc, -1)
    sum_h = jnp.sum(sum_h, -1)[:, :heads]
    pieces = [sum_x, grad_norm_w, sum_h, grad_gain]
    flat = jnp.concatenate([p.reshape(-1) for p in pieces] + [sum_bc.reshape(-1)])
    size = flat.shape[0]
    flat = jnp.pad(flat, (0, -size % 1024)).reshape(-1, LANES)
    flat = sum_over(flat, ctx_bits + dp_bits).reshape(-1)[:size]
    out = []
    for p in pieces + [sum_bc]:
        out.append(flat[: p.size].reshape(p.shape))
        flat = flat[p.size :]
    sum_x, grad_norm_w, sum_h, grad_gain, sum_bc = out
    sum_bc = sum_over(sum_bc, tensor_bits)
    taps = conv_x_w.shape[0]
    row = lax.axis_index("dp") * lax.axis_size("ctx") + lax.axis_index("ctx")
    grad_gain = lax.dynamic_slice_in_dim(
        grad_gain, row * norm_gain.shape[0], norm_gain.shape[0], 0
    )
    return (
        mixed_out,
        grad_tokens,
        grad_gain,
        jnp.stack([grad_w_gate, grad_w_inner], 1),
        grad_w_dt,
        grad_w_bc,
        sum_x[:taps],
        sum_x[taps],
        sum_bc[:taps],
        sum_bc[taps],
        sum_h[0],
        sum_h[1],
        sum_h[2],
        grad_norm_w,
        grad_w_out,
    )


def solution(mesh):
    rows = P(("dp", "ctx"), "tensor")
    tokens = P("dp", "ctx", None)
    heads = P("tensor")
    return jax.shard_map(
        per_device,
        mesh=mesh,
        in_specs=(
            tokens, P(("dp", "ctx")), P(("dp", "ctx"), None, "tensor"), rows, P(("dp", "ctx"), None),
            P(None, "tensor"), heads, P(), P(), heads, heads, heads, heads, rows, tokens,
        ),
        out_specs=(
            tokens, tokens, P(("dp", "ctx")), P(("dp", "ctx"), None, "tensor"), rows,
            P(("dp", "ctx"), None), P(None, "tensor"), heads, P(), P(), heads, heads, heads, heads, rows,
        ),
        check_vma=False,
    )
```

```python
from functools import partial

import jax
import jax.numpy as jnp
from jax import lax
from jax.experimental import pallas as pl
from jax.experimental.pallas import tpu as pltpu
from jax.sharding import PartitionSpec as P

EPS = 1e-05
LOG2E = 1.4426950408889634
LANES = 128
GROUP = 2
HIGH = lax.Precision.HIGHEST
BF = jnp.bfloat16
F32 = jnp.float32


def bits_of(axis):
    return [1 << i for i in reversed(range(lax.axis_size(axis).bit_length() - 1))]


def swap(block, axis, mask):
    return lax.ppermute(block, axis, [(i, i ^ mask) for i in range(lax.axis_size(axis))])


def side(axis, bit):
    return (lax.axis_index(axis) // bit) % 2


def row_bits():
    return [("dp", b) for b in bits_of("dp")] + [("ctx", b) for b in bits_of("ctx")]


def open_gather(shard):
    return shard.reshape((1,) * len(row_bits()) + shard.shape)


def double(whole, place):
    dim = row_bits().index(place)
    other = swap(whole, *place)
    return jnp.where(
        side(*place) == 1,
        jnp.concatenate([other, whole], dim),
        jnp.concatenate([whole, other], dim),
    )


def close_gather(whole):
    return whole.reshape((-1,) + whole.shape[len(row_bits()) + 1 :])


def gather_rows(shard, order):
    whole = open_gather(shard)
    for place in order:
        whole = double(whole, place)
    return close_gather(whole)


def both_ways(array, cut):
    return [array[:, :cut], array[:, cut:]]


def tie(*trees):
    leaves, shape = jax.tree.flatten(trees)
    return jax.tree.unflatten(shape, lax.optimization_barrier(tuple(leaves)))


def offer(part, dim, axis):
    me = lax.axis_index(axis)
    pieces = [
        lax.dynamic_index_in_dim(part, me ^ k, dim, False) for k in range(lax.axis_size(axis))
    ]
    return [swap(x, axis, k) if k else x for k, x in enumerate(pieces)]


def add_up(pieces):
    return sum(x.astype(F32) for x in pieces)


def open_scatter(part):
    return part.reshape((lax.axis_size("dp"), lax.axis_size("ctx"), -1) + part.shape[1:])


def sum_over(part, places):
    for place in places:
        part = part + swap(part, *place)
    return part


def spread_out(blocks, length):
    parts = lax.axis_size("ctx")
    me = lax.axis_index("ctx")
    cuts = lax.axis_size("tensor")
    rows = length // cuts
    width = blocks.shape[-1]
    seqs = blocks.shape[0] // parts
    mine = lax.dynamic_slice_in_dim(blocks, lax.axis_index("tensor") * rows, rows, 1)
    mine = mine.reshape(parts, seqs, rows, width)
    slots = []
    for k in range(parts):
        piece = lax.dynamic_index_in_dim(mine, me ^ k, 0, False)
        slots.append(swap(piece, "ctx", k) if k else piece)
    return slots


def gather_cuts(share):
    for bit in reversed(bits_of("tensor")):
        other = swap(share, "tensor", bit)
        share = jnp.where(
            side("tensor", bit) == 1,
            jnp.concatenate([other, share], 2),
            jnp.concatenate([share, other], 2),
        )
    return share


def shares(grad, weight):
    cuts = lax.axis_size("tensor")
    rows = grad.shape[3] // cuts
    me = lax.axis_index("tensor")
    return [
        project_back(lax.dynamic_slice_in_dim(grad, (me ^ k) * rows, rows, 3), weight)
        for k in range(cuts)
    ]


def own_share(parts):
    mine, *others = parts
    return mine + add_up([swap(x.astype(BF), "tensor", k + 1) for k, x in enumerate(others)])


def send_home(share):
    return [swap(share[k], "ctx", k) if k else share[k] for k in range(lax.axis_size("ctx"))]


def arrange(slots):
    me = lax.axis_index("ctx")
    home = gather_cuts(jnp.stack(slots))
    home = jnp.concatenate([lax.dynamic_index_in_dim(home, me ^ k, 0) for k in range(len(slots))])
    return home.reshape((-1,) + home.shape[2:])


def dot(a, b, dims):
    return lax.dot_general(a, b, (dims, ((), ())), preferred_element_type=F32)


NN = ((1,), (0,))
NT = ((1,), (1,))
TN = ((0,), (0,))


def tiled(lanes, width):
    return jnp.concatenate([lanes] * (width // lanes.shape[1]), 1)


def conv_rows(raw, before, weight):
    taps = len(weight) - 1
    width = raw.shape[1]
    ext = jnp.concatenate([before, raw], 1)
    total = tiled(weight[taps], width) + tiled(weight[taps - 1], width) * raw
    for k in range(1, taps):
        total += tiled(weight[taps - 1 - k], width) * pltpu.roll(ext, k, 1)[:, LANES:]
    return total


def fold(rows):
    return sum(rows[:, i : i + LANES] for i in range(0, rows.shape[1], LANES))


def conv_back(grad, after, raw, weight):
    taps = len(weight) - 1
    width = grad.shape[1]
    ext = jnp.concatenate([grad, after], 1)
    out = tiled(weight[taps - 1], width) * grad
    terms = [None] * (taps - 1) + [fold(grad * raw), fold(grad)]
    for k in range(1, taps):
        moved = pltpu.roll(ext, width + LANES - k, 1)[:, :width]
        out += tiled(weight[taps - 1 - k], width) * moved
        terms[taps - 1 - k] = fold(moved * raw)
    return out, terms


def order_mask(width, keep):
    row = lax.broadcasted_iota(jnp.int32, (width, width), 0)
    col = lax.broadcasted_iota(jnp.int32, (width, width), 1)
    return keep(row, col)


def head_rows(dt_raw, dt_bias, a_log):
    biased = dt_raw + dt_bias
    step = jnp.maximum(biased, 0.0) + jnp.log1p(jnp.exp(-jnp.abs(biased)))
    a_decay = -jnp.exp(a_log)
    return biased, step, a_decay


def fill_heads(cs, heads, cs_ref, col_ref, ecs_ref, rem_ref, end_ref):
    width = cs.shape[1]
    cs2 = cs * LOG2E
    cs_ref[...] = cs2
    last = jnp.broadcast_to(cs2[:, width - 1 :], cs2.shape)
    ecs_ref[...] = jnp.exp2(cs2)
    rem_ref[...] = jnp.exp2(last - cs2)
    end_ref[...] = jnp.exp2(last[:, :LANES])
    columns = jnp.transpose(cs2)
    for h in range(heads):
        col_ref[h] = jnp.broadcast_to(columns[:, h : h + 1], (width, LANES))


def decay_blocks(cs_row, column):
    count = cs_row.shape[1] // LANES
    out = {}
    for i in range(count):
        for j in range(i, count):
            gap = cs_row[:, j * LANES : (j + 1) * LANES] - column[i * LANES : (i + 1) * LANES]
            out[i, j] = jnp.exp2(jnp.minimum(gap, 0.0) if i == j else gap)
    return out


def block(ref, i, j):
    return ref[i * LANES : (i + 1) * LANES, j * LANES : (j + 1) * LANES]


def mixing(decay, score_ref):
    count = score_ref.shape[0] // LANES
    none = jnp.zeros((LANES, LANES), BF)
    return jnp.concatenate(
        [
            jnp.concatenate(
                [
                    (decay[i, j] * block(score_ref, i, j)).astype(BF) if j >= i else none
                    for j in range(count)
                ],
                1,
            )
            for i in range(count)
        ],
        0,
    )


def loop_heads(heads, compute, store):
    group = GROUP if heads % GROUP == 0 else 1

    def some(i, carry):
        done = [compute(i * group + u) for u in range(group)]
        store(done)
        return carry

    lax.fori_loop(0, heads // group, some, 0)


def forward_kernel(
    heads, me, raw, bc_raw, dt_raw, cw, cbw, hp,
    z_out, y_out, cs_out, mem_out, zbc_out,
    mem, before, before_bc, step_s, cs_s, col_s, ecs_s, rem_s, end_s, score_s, maps_s,
):
    head_size = raw.shape[2] // heads
    half = bc_raw.shape[2] // 2
    width = raw.shape[3]
    taps = cw.shape[0]

    @pl.when(pl.program_id(1) == 0)
    def _():
        mem[...] = jnp.zeros_like(mem)
        before[...] = jnp.zeros_like(before)
        before_bc[...] = jnp.zeros_like(before_bc)

    bc = bc_raw[0, 0].astype(F32)
    zbc = conv_rows(bc, before_bc[...], [cbw[j] for j in range(taps)])
    before_bc[...] = bc[:, width - LANES :]
    zbc_out[0, 0] = zbc
    maps_s[...] = (zbc * jax.nn.sigmoid(zbc)).astype(BF)
    causal = order_mask(width, lambda s, t: s <= t)
    score_s[...] = jnp.where(causal, dot(maps_s[:half], maps_s[half:], TN), 0.0)

    _, step, a_decay = head_rows(dt_raw[0, 0], hp[0], hp[1])
    cs = jnp.dot(step * a_decay, causal.astype(F32), precision=HIGH, preferred_element_type=F32)
    cs_out[0, 0] = cs
    step_s[...] = step
    fill_heads(cs, heads, cs_s, col_s, ecs_s, rem_s, end_s)

    def compute(h):
        rows = pl.ds(pl.multiple_of(h * head_size, head_size), head_size)
        row = pl.ds(h, 1)
        own = raw[0, 0, rows, :].astype(F32)
        z = conv_rows(own, before[rows, :], [cw[j, rows, :] for j in range(taps)])
        x = z * jax.nn.sigmoid(z)
        scaled = x * step_s[row, :]
        decay = decay_blocks(cs_s[row, :], col_s[h])
        inside = dot(scaled.astype(BF), mixing(decay, score_s), NN)
        memory = mem[rows, :]
        memory_low = memory.astype(BF)
        held = dot(memory_low, maps_s[half:], NN) * ecs_s[row, :]
        y = inside + held + hp[2, row, :] * x
        gained = dot((scaled * rem_s[row, :]).astype(BF), maps_s[:half], NT)
        return rows, own[:, width - LANES :], z, y, memory_low, memory * end_s[row, :] + gained

    def store(done):
        for rows, edge, z, y, memory_low, memory in done:
            before[rows, :] = edge
            z_out[0, 0, rows, :] = z
            y_out[0, 0, rows, :] = y
            mem_out[0, 0, rows, :] = memory_low
            mem[rows, :] = memory

    loop_heads(heads, compute, store)


def backward_kernel(
    heads, me, z_in, raw, y_in, g_in, zbc_in, bc_raw, dt_raw, cs_in, mem_in, cw, cbw, hp,
    grad_out, sum_x, sum_bc, sum_h,
    gmem, gmem_low, after, after_bc, step_s, cs_s, col_s, ecs_s, rem_s, end_s, score_s, maps_s,
    gscore_s, eg_s, rx_s, pq_s, e_s, r_s, d_s, k_s,
):
    inner = raw.shape[2]
    head_size = inner // heads
    half = zbc_in.shape[2] // 2
    width = raw.shape[3]
    taps = cw.shape[0]

    @pl.when((pl.program_id(0) == 0) & (pl.program_id(1) == 0))
    def _():
        sum_x[...] = jnp.zeros_like(sum_x)
        sum_h[...] = jnp.zeros_like(sum_h)
        pq_s[...] = jnp.zeros_like(pq_s)
        e_s[...] = jnp.zeros_like(e_s)
        r_s[...] = jnp.zeros_like(r_s)
        d_s[...] = jnp.zeros_like(d_s)
        k_s[...] = jnp.zeros_like(k_s)
        sum_bc[...] = jnp.zeros_like(sum_bc)

    @pl.when(pl.program_id(1) == 0)
    def _():
        gmem[...] = jnp.zeros_like(gmem)
        after[...] = jnp.zeros_like(after)
        after_bc[...] = jnp.zeros_like(after_bc)

    zbc = zbc_in[0, 0]
    sig_bc = jax.nn.sigmoid(zbc)
    maps_s[...] = (zbc * sig_bc).astype(BF)
    causal = order_mask(width, lambda s, t: s <= t)
    score_s[...] = jnp.where(causal, dot(maps_s[:half], maps_s[half:], TN), 0.0)
    gscore_s[...] = jnp.zeros_like(gscore_s)

    biased, step, a_decay = head_rows(dt_raw[0, 0], hp[0], hp[1])
    step_s[...] = step
    fill_heads(cs_in[0, 0], heads, cs_s, col_s, ecs_s, rem_s, end_s)

    def compute(h):
        rows = pl.ds(pl.multiple_of(h * head_size, head_size), head_size)
        row = pl.ds(h, 1)
        z = z_in[0, 0, rows, :]
        sig = jax.nn.sigmoid(z)
        x = z * sig
        step_row = step_s[row, :]
        skip = hp[2, row, :]
        scaled = x * step_row
        scaled_low = scaled.astype(BF)
        scaled_back = scaled_low.astype(F32)
        g_low = g_in[0, 0, rows, :]
        g = g_low.astype(F32)
        decay = decay_blocks(cs_s[row, :], col_s[h])
        inside = dot(g_low, mixing(decay, score_s), NT)
        gweights = dot(scaled_low, g_low, TN)
        gscore = {
            (i, j): weight * gweights[i * LANES : (i + 1) * LANES, j * LANES : (j + 1) * LANES]
            for (i, j), weight in decay.items()
        }
        later = gmem[rows, :]
        later_low = later.astype(BF)
        outside = dot(later_low, maps_s[:half], NN) * rem_s[row, :]
        gscaled = inside + outside
        both = g * (y_in[0, 0, rows, :] - skip * x) - scaled_back * inside
        sums = (
            jnp.sum(both, 0, keepdims=True),
            jnp.sum(scaled_back * outside, 0, keepdims=True),
            jnp.sum(x * gscaled, 0, keepdims=True),
            d_s[row, :] + jnp.sum(g * x, 0, keepdims=True),
            jnp.sum(later * mem_in[0, 0, rows, :].astype(F32), 0, keepdims=True),
        )
        eg = (g * ecs_s[row, :]).astype(BF)
        rx = (scaled * rem_s[row, :]).astype(BF)
        earlier = later * end_s[row, :] + dot(eg, maps_s[half:], NT)
        gz = (step_row * gscaled + skip * g) * (sig * (1.0 + z * (1.0 - sig)))
        grad, terms = conv_back(
            gz, after[rows, :], raw[0, 0, rows, :].astype(F32),
            [cw[j, rows, :] for j in range(taps)],
        )
        terms = [sum_x[j, rows, :] + term for j, term in enumerate(terms)]
        return rows, row, gscore, sums, later_low, eg, rx, earlier, gz[:, :LANES], grad, terms

    def store(done):
        for i, j in done[0][2]:
            place = (slice(i * LANES, (i + 1) * LANES), slice(j * LANES, (j + 1) * LANES))
            gscore_s[place] += sum(one[2][i, j] for one in done)
        for rows, row, _, sums, later_low, eg, rx, earlier, edge, grad, terms in done:
            for ref, value in zip((pq_s, e_s, r_s, d_s, k_s), sums):
                ref[row, :] = value
            gmem_low[rows, :] = later_low
            eg_s[rows, :] = eg
            rx_s[rows, :] = rx
            gmem[rows, :] = earlier
            after[rows, :] = edge
            grad_out[0, 0, rows, :] = grad.astype(BF)
            for j, term in enumerate(terms):
                sum_x[j, rows, :] = term

    loop_heads(heads, compute, store)

    gscore = jnp.where(causal, gscore_s[...], 0.0).astype(BF)
    gout_map = dot(maps_s[:half], gscore, NN) + dot(mem_in[0, 0], eg_s[...], TN)
    gin_map = dot(maps_s[half:], gscore, NT) + dot(gmem_low[...], rx_s[...], TN)
    gmaps = jnp.concatenate([gin_map, gout_map], 0) * (sig_bc * (1.0 + zbc * (1.0 - sig_bc)))
    gbc, terms = conv_back(
        gmaps, after_bc[...], bc_raw[0, 0].astype(F32), [cbw[j] for j in range(taps)]
    )
    for j, term in enumerate(terms):
        sum_bc[j] += term
    after_bc[...] = gmaps[:, :LANES]
    grad_out[0, 0, inner : inner + 2 * half, :] = gbc.astype(BF)

    from_here = order_mask(width, lambda t, u: t >= u).astype(F32)
    strictly = order_mask(width, lambda s, u: s < u).astype(F32)
    carried = jnp.sum(k_s[...], 1, keepdims=True) * end_s[:, :1]
    gdecay = (
        jnp.dot(pq_s[...], from_here, precision=HIGH, preferred_element_type=F32)
        + jnp.dot(e_s[...], strictly, precision=HIGH, preferred_element_type=F32)
        + carried
    )
    gdt = (a_decay * gdecay + r_s[...]) * jax.nn.sigmoid(biased)
    grad_out[0, 0, inner + 2 * half :, :] = gdt.astype(BF)
    sum_h[0] += fold(gdt)
    sum_h[1] += fold(gdecay * step * a_decay)

    @pl.when((pl.program_id(0) == pl.num_programs(0) - 1) & (pl.program_id(1) == pl.num_programs(1) - 1))
    def _():
        sum_h[2] = fold(d_s[...])


def head_scratch(head_pad, heads, width, maps):
    return [
        pltpu.VMEM((head_pad, width), F32),
        pltpu.VMEM((head_pad, width), F32),
        pltpu.VMEM((heads, width, LANES), F32),
        pltpu.VMEM((head_pad, width), F32),
        pltpu.VMEM((head_pad, width), F32),
        pltpu.VMEM((head_pad, LANES), F32),
        pltpu.VMEM((width, width), F32),
        pltpu.VMEM((maps, width), BF),
    ]


def fixed(array):
    return pl.BlockSpec(array.shape, lambda s, c, me: (0,) * len(array.shape))


def kernel_call(body, name, flops, reverse, inputs, kinds, outs, scratch):
    parts, seqs = inputs[0].shape[:2]

    def part(array):
        def place(s, c, me):
            return ((parts - 1 - c if reverse else c) ^ me[0], s, 0, 0)

        return pl.BlockSpec((1, 1) + array.shape[2:], place)

    def spec(array, kind):
        return part(array) if kind == "p" else fixed(array)

    return pl.pallas_call(
        body,
        grid_spec=pltpu.PrefetchScalarGridSpec(
            num_scalar_prefetch=1,
            grid=(seqs, parts),
            in_specs=[spec(x, k) for x, k in zip(inputs, kinds)],
            out_specs=[spec(x, k) for x, k in outs],
            scratch_shapes=scratch,
        ),
        out_shape=[x for x, _ in outs],
        compiler_params=pltpu.CompilerParams(
            dimension_semantics=("arbitrary", "arbitrary"), vmem_limit_bytes=48 << 20
        ),
        cost_estimate=pl.CostEstimate(flops=flops, bytes_accessed=16 << 20, transcendentals=0),
        name=name,
    )(lax.axis_index("ctx").reshape(1), *inputs)


def run_forward(inner, bc, dt, cw, cbw, hp, heads):
    parts, seqs, rows, width = inner.shape
    maps, head_pad, states = bc.shape[2], dt.shape[2], bc.shape[2] // 2

    def out(count, last=width, kind=F32):
        return jax.ShapeDtypeStruct((parts, seqs, count, last), kind), "p"

    scratch = [
        pltpu.VMEM((rows, states), F32), pltpu.VMEM((rows, LANES), F32), pltpu.VMEM((maps, LANES), F32),
    ]
    return kernel_call(
        partial(forward_kernel, heads), "scan_forward", 45 << 30, False,
        [inner, bc, dt, cw, cbw, hp], "pppfff",
        [out(rows), out(rows), out(head_pad), out(rows, states, BF), out(maps)],
        scratch + head_scratch(head_pad, heads, width, maps),
    )


def run_backward(z, inner, y, g, zbc, bc, dt, cs, mem, cw, cbw, hp, heads):
    parts, seqs, rows, width = inner.shape
    maps, head_pad, states = zbc.shape[2], dt.shape[2], zbc.shape[2] // 2
    grads = jax.ShapeDtypeStruct((parts, seqs, rows + maps + head_pad, width), BF)
    sums = [cw.shape, cbw.shape, (3, head_pad, LANES)]
    scratch = [
        pltpu.VMEM((rows, states), F32), pltpu.VMEM((rows, states), BF),
        pltpu.VMEM((rows, LANES), F32), pltpu.VMEM((maps, LANES), F32),
    ]
    scratch += head_scratch(head_pad, heads, width, maps)
    scratch += [
        pltpu.VMEM((width, width), F32), pltpu.VMEM((rows, width), BF), pltpu.VMEM((rows, width), BF),
    ]
    scratch += [pltpu.VMEM((head_pad, width), F32)] * 4 + [pltpu.VMEM((head_pad, LANES), F32)]
    return kernel_call(
        partial(backward_kernel, heads), "scan_backward", 60 << 30, True,
        [z, inner, y, g, zbc, bc, dt, cs, mem, cw, cbw, hp], "pppppppppfff",
        [(grads, "p")] + [(jax.ShapeDtypeStruct(x, F32), "f") for x in sums], scratch,
    )


def project(rows, weight):
    return jnp.einsum("ksld,di->ksil", rows, weight, preferred_element_type=F32)


def project_back(grad, weight):
    return jnp.einsum("ksil,di->ksld", grad, weight, preferred_element_type=F32)


def weight_grad(rows, grad):
    return jnp.einsum("ksld,ksil->di", rows, grad, preferred_element_type=F32)


def per_device(
    tokens, norm_gain, w_zx, w_dt, w_bc, conv_x_w, conv_x_b, conv_bc_w, conv_bc_b,
    dt_bias, a_log, d_skip, norm_w, w_out, output_gradient,
):
    seqs_here, length, width = tokens.shape
    heads = w_dt.shape[1]
    head_pad = -(-heads // 16) * 16
    inner_here = w_out.shape[1]
    inner_total = inner_here * lax.axis_size("tensor")
    maps = w_bc.shape[1]
    rest = inner_here + maps
    dp_bits = [("dp", b) for b in bits_of("dp")]
    ctx_bits = [("ctx", b) for b in bits_of("ctx")]
    ways = [ctx_bits, ctx_bits[::-1]]
    tensor_bits = [("tensor", b) for b in bits_of("tensor")]

    rows = spread_out(tokens, length)
    scan_weights = jnp.concatenate(
        [w_zx[:, 1], w_bc, jnp.pad(w_dt, ((0, 0), (0, head_pad - heads)))], 1
    )
    scan_weights = both_ways(scan_weights, inner_here // 2 + LANES)
    full_scan = jnp.concatenate(
        [gather_rows(x, dp_bits + way) for x, way in zip(scan_weights, ways)], 1
    )
    gain = gather_rows(norm_gain[None], dp_bits + ctx_bits).reshape(-1).astype(F32)
    rows = gather_cuts(jnp.stack(rows))
    rows, gain, outer, cot_ready = tie(
        rows, gain, jnp.concatenate([w_out, w_zx[:, 0]], 1), output_gradient
    )
    outer = lax.all_gather(outer, ("dp", "ctx"), axis=0, tiled=True)
    cots = spread_out(cot_ready, length)

    def lanes(column):
        return jnp.broadcast_to(column[..., None], column.shape + (LANES,))

    cw = lanes(jnp.concatenate([conv_x_w, conv_x_b[None]], 0))
    cbw = lanes(jnp.concatenate([conv_bc_w, conv_bc_b[None]], 0))
    hp = jnp.pad(jnp.stack([dt_bias, a_log, d_skip]), ((0, 0), (0, head_pad - heads)))
    hp = jnp.broadcast_to(hp[..., None], hp.shape + (length,))

    residual = rows.astype(F32)
    normed = (
        residual * lax.rsqrt(jnp.mean(residual * residual, axis=-1, keepdims=True) + EPS) * gain
    ).astype(BF)
    inner_raw = project(normed, full_scan[:, :inner_here]).astype(BF)
    bc_raw = project(normed, full_scan[:, inner_here:rest]).astype(BF)
    dt_raw = project(normed, full_scan[:, rest:])
    z, y, cs, mem, zbc = run_forward(inner_raw, bc_raw, dt_raw, cw, cbw, hp, heads)

    y, outer, cots = tie(y, outer, cots)
    cots = gather_cuts(jnp.stack(cots))
    full_out, full_gate = outer[:, :inner_here], outer[:, inner_here:]
    norm_column = norm_w[:, None]
    gate_raw = project(normed, full_gate)
    grad_mixed = project(cots, full_out)
    gate_sig = jax.nn.sigmoid(gate_raw)
    gate_act = gate_raw * gate_sig
    gated = y * gate_act
    weighted = grad_mixed * norm_column
    sums = jnp.stack([jnp.sum(gated * gated, axis=2), jnp.sum(weighted * gated, axis=2)])
    sums = sum_over(sums, tensor_bits)[:, :, :, None]
    inv_rms = lax.rsqrt(sums[0] / inner_total + EPS)
    mixed_in = (gated * inv_rms * norm_column).astype(BF)
    grad_norm_w = jnp.sum(grad_mixed * gated * inv_rms, axis=(0, 1, 3))
    grad_gated = inv_rms * weighted - gated * (inv_rms * inv_rms * inv_rms) * (
        sums[1] / inner_total
    )
    grad_gate = (grad_gated * y * gate_sig * (1.0 + gate_raw * (1.0 - gate_sig))).astype(BF)
    grad_y = (grad_gated * gate_act).astype(BF)

    outer_grad = jnp.concatenate(
        [weight_grad(cots, mixed_in).astype(BF), weight_grad(normed, grad_gate).astype(BF)], 1
    )
    mixed_in, grad_gate, outer_grad = tie(mixed_in, grad_gate, outer_grad)
    outer_grad = offer(open_scatter(outer_grad), 1, "ctx")
    cuts = lax.axis_size("tensor")
    share = lax.dynamic_slice_in_dim(
        rows, lax.axis_index("tensor") * (length // cuts), length // cuts, 2
    ).astype(F32)
    mixed = (share + own_share(shares(mixed_in, full_out))).astype(BF)
    normed_gate = [x.astype(BF) for x in shares(grad_gate, full_gate)]
    grad_y, mixed, normed_gate = tie(grad_y, mixed, normed_gate)
    mixed = send_home(mixed)

    grad_scan, sum_x, sum_bc, sum_h = run_backward(
        z, inner_raw, y, grad_y, zbc, bc_raw, dt_raw, cs, mem, cw, cbw, hp, heads
    )
    grad_scan, mixed, outer_grad = tie(grad_scan, mixed, outer_grad)

    scan_grad = weight_grad(normed, grad_scan).astype(BF)
    grad_scan, scan_grad = tie(grad_scan, scan_grad)
    scan_grad = offer(open_scatter(scan_grad), 1, "ctx")
    grad_share = [
        x.astype(F32) + part for x, part in zip(normed_gate, shares(grad_scan, full_scan))
    ]
    grad_share = own_share(grad_share).astype(BF)
    grad_share, scan_grad, outer_grad = tie(grad_share, scan_grad, outer_grad)
    grad_home = send_home(grad_share)
    weight_grads = jnp.concatenate([add_up(outer_grad), add_up(scan_grad)], -1).astype(BF)
    weight_grads = add_up(offer(weight_grads, 0, "dp"))
    grad_w_out, grad_w_gate = weight_grads[:, :inner_here], weight_grads[:, inner_here : 2 * inner_here]
    scan_grad = weight_grads[:, 2 * inner_here :]
    grad_w_inner = scan_grad[:, :inner_here]
    grad_w_bc = sum_over(scan_grad[:, inner_here:rest], tensor_bits)
    grad_w_dt = scan_grad[:, rest : rest + heads]
    r = lax.rsqrt(jnp.mean(share * share, axis=-1, keepdims=True) + EPS)
    grad_gain = jnp.sum(share * r * grad_share.astype(F32), axis=(0, 1, 2))

    sum_x = jnp.sum(sum_x, -1)
    sum_bc = jnp.sum(sum_bc, -1)
    sum_h = jnp.sum(sum_h, -1)[:, :heads]
    pieces = [sum_x, grad_norm_w, sum_h, grad_gain, sum_bc]
    flat = jnp.concatenate([p.reshape(-1) for p in pieces])
    size = flat.shape[0]
    flat = jnp.pad(flat, (0, -size % 1024)).reshape(-1, LANES)
    flat = sum_over(flat, ctx_bits + dp_bits).reshape(-1)[:size]
    out = []
    for p in pieces:
        out.append(flat[: p.size].reshape(p.shape))
        flat = flat[p.size :]
    sum_x, grad_norm_w, sum_h, grad_gain, sum_bc = out
    sum_bc, grad_gain = jax.tree.map(lambda x: sum_over(x, tensor_bits), (sum_bc, grad_gain))
    taps = conv_x_w.shape[0]
    row = lax.axis_index("dp") * lax.axis_size("ctx") + lax.axis_index("ctx")
    grad_gain = lax.dynamic_slice_in_dim(
        grad_gain, row * norm_gain.shape[0], norm_gain.shape[0], 0
    )

    mixed_out = arrange(mixed)
    grad_home = arrange(grad_home).astype(F32)
    here = tokens.astype(F32)
    r = lax.rsqrt(jnp.mean(here * here, axis=-1, keepdims=True) + EPS)
    scaled = gain * grad_home
    grad_tokens = (
        output_gradient.astype(F32)
        + r * scaled
        - here * (r * r * r) * jnp.mean(here * scaled, axis=-1, keepdims=True)
    )
    return (
        mixed_out,
        grad_tokens,
        grad_gain,
        jnp.stack([grad_w_gate, grad_w_inner], 1),
        grad_w_dt,
        grad_w_bc,
        sum_x[:taps],
        sum_x[taps],
        sum_bc[:taps],
        sum_bc[taps],
        sum_h[0],
        sum_h[1],
        sum_h[2],
        grad_norm_w,
        grad_w_out,
    )


def solution(mesh):
    rows = P(("dp", "ctx"), "tensor")
    tokens = P("dp", "ctx", None)
    heads = P("tensor")
    return jax.shard_map(
        per_device,
        mesh=mesh,
        in_specs=(
            tokens, P(("dp", "ctx")), P(("dp", "ctx"), None, "tensor"), rows, P(("dp", "ctx"), None),
            P(None, "tensor"), heads, P(), P(), heads, heads, heads, heads, rows, tokens,
        ),
        out_specs=(
            tokens, tokens, P(("dp", "ctx")), P(("dp", "ctx"), None, "tensor"), rows,
            P(("dp", "ctx"), None), P(None, "tensor"), heads, P(), P(), heads, heads, heads, heads, rows,
        ),
        check_vma=False,
    )
```

```python
from functools import partial

import jax
import jax.numpy as jnp
from jax import lax
from jax.experimental import pallas as pl
from jax.experimental.pallas import tpu as pltpu
from jax.sharding import PartitionSpec as P

EPS = 1e-05
LOG2E = 1.4426950408889634
LANES = 128
GROUP = 4
HIGH = lax.Precision.HIGHEST
BF = jnp.bfloat16
F32 = jnp.float32


def bits_of(axis):
    return [1 << i for i in reversed(range(lax.axis_size(axis).bit_length() - 1))]


def swap(block, axis, mask):
    return lax.ppermute(block, axis, [(i, i ^ mask) for i in range(lax.axis_size(axis))])


def side(axis, bit):
    return (lax.axis_index(axis) // bit) % 2


def row_bits():
    return [("dp", b) for b in bits_of("dp")] + [("ctx", b) for b in bits_of("ctx")]


def open_gather(shard):
    return shard.reshape((1,) * len(row_bits()) + shard.shape)


def double(whole, place):
    dim = row_bits().index(place)
    other = swap(whole, *place)
    return jnp.where(
        side(*place) == 1,
        jnp.concatenate([other, whole], dim),
        jnp.concatenate([whole, other], dim),
    )


def close_gather(whole):
    return whole.reshape((-1,) + whole.shape[len(row_bits()) + 1 :])


def both_ways(array, cut):
    return [array[:, :cut], array[:, cut:]]


def tie(*trees):
    leaves, shape = jax.tree.flatten(trees)
    return jax.tree.unflatten(shape, lax.optimization_barrier(tuple(leaves)))


def offer(part, dim, axis):
    me = lax.axis_index(axis)
    pieces = [
        lax.dynamic_index_in_dim(part, me ^ k, dim, False) for k in range(lax.axis_size(axis))
    ]
    return [swap(x, axis, k) if k else x for k, x in enumerate(pieces)]


def add_up(pieces):
    return sum(x.astype(F32) for x in pieces)


def scatter_dp(part):
    bits = bits_of("dp")
    left = part.reshape((2,) * len(bits) + part.shape[1:])
    for dim, bit in reversed(list(enumerate(bits))):
        up = side("dp", bit)
        mine = lax.dynamic_index_in_dim(left, up, dim)
        theirs = lax.dynamic_index_in_dim(left, 1 - up, dim)
        left = mine + swap(theirs.astype(BF), "dp", bit).astype(F32)
    return left.reshape(part.shape[1:])


def open_scatter(part):
    return part.reshape((lax.axis_size("dp"), lax.axis_size("ctx"), -1) + part.shape[1:])


def sum_over(part, places):
    for place in places:
        part = part + swap(part, *place)
    return part


def spread_out(blocks, length):
    parts = lax.axis_size("ctx")
    me = lax.axis_index("ctx")
    cuts = lax.axis_size("tensor")
    rows = length // cuts
    width = blocks.shape[-1]
    seqs = blocks.shape[0] // parts
    mine = lax.dynamic_slice_in_dim(blocks, lax.axis_index("tensor") * rows, rows, 1)
    mine = mine.reshape(parts, seqs, rows, width)
    slots = []
    for k in range(parts):
        piece = lax.dynamic_index_in_dim(mine, me ^ k, 0, False)
        slots.append(swap(piece, "ctx", k) if k else piece)
    return slots


def gather_cuts(share):
    for bit in reversed(bits_of("tensor")):
        other = swap(share, "tensor", bit)
        share = jnp.where(
            side("tensor", bit) == 1,
            jnp.concatenate([other, share], 2),
            jnp.concatenate([share, other], 2),
        )
    return share


def shares(grad, weight):
    cuts = lax.axis_size("tensor")
    rows = grad.shape[3] // cuts
    me = lax.axis_index("tensor")
    return [
        project_back(lax.dynamic_slice_in_dim(grad, (me ^ k) * rows, rows, 3), weight)
        for k in range(cuts)
    ]


def own_share(parts):
    mine, *others = parts
    return mine + add_up([swap(x.astype(BF), "tensor", k + 1) for k, x in enumerate(others)])


def send_home(share):
    return [swap(share[k], "ctx", k) if k else share[k] for k in range(lax.axis_size("ctx"))]


def arrange(slots):
    me = lax.axis_index("ctx")
    home = gather_cuts(jnp.stack(slots))
    home = jnp.concatenate([lax.dynamic_index_in_dim(home, me ^ k, 0) for k in range(len(slots))])
    return home.reshape((-1,) + home.shape[2:])


def dot(a, b, dims):
    return lax.dot_general(a, b, (dims, ((), ())), preferred_element_type=F32)


NN = ((1,), (0,))
NT = ((1,), (1,))
TN = ((0,), (0,))


def tiled(lanes, width):
    return jnp.concatenate([lanes] * (width // lanes.shape[1]), 1)


def conv_rows(raw, before, weight):
    taps = len(weight) - 1
    width = raw.shape[1]
    ext = jnp.concatenate([before, raw], 1)
    total = tiled(weight[taps], width) + tiled(weight[taps - 1], width) * raw
    for k in range(1, taps):
        total += tiled(weight[taps - 1 - k], width) * pltpu.roll(ext, k, 1)[:, LANES:]
    return total


def fold(rows):
    return sum(rows[:, i : i + LANES] for i in range(0, rows.shape[1], LANES))


def conv_back(grad, after, raw, weight):
    taps = len(weight) - 1
    width = grad.shape[1]
    ext = jnp.concatenate([grad, after], 1)
    out = tiled(weight[taps - 1], width) * grad
    terms = [None] * (taps - 1) + [fold(grad * raw), fold(grad)]
    for k in range(1, taps):
        moved = pltpu.roll(ext, width + LANES - k, 1)[:, :width]
        out += tiled(weight[taps - 1 - k], width) * moved
        terms[taps - 1 - k] = fold(moved * raw)
    return out, terms


def order_mask(width, keep):
    row = lax.broadcasted_iota(jnp.int32, (width, width), 0)
    col = lax.broadcasted_iota(jnp.int32, (width, width), 1)
    return keep(row, col)


def head_rows(dt_raw, dt_bias, a_log):
    biased = dt_raw + dt_bias
    step = jnp.maximum(biased, 0.0) + jnp.log1p(jnp.exp(-jnp.abs(biased)))
    a_decay = -jnp.exp(a_log)
    return biased, step, a_decay


def fill_heads(cs, heads, cs_ref, col_ref, ecs_ref, rem_ref, end_ref):
    width = cs.shape[1]
    cs2 = cs * LOG2E
    cs_ref[...] = cs2
    last = jnp.broadcast_to(cs2[:, width - 1 :], cs2.shape)
    ecs_ref[...] = jnp.exp2(cs2)
    rem_ref[...] = jnp.exp2(last - cs2)
    end_ref[...] = jnp.exp2(last[:, :LANES])
    columns = jnp.transpose(cs2)
    for h in range(heads):
        col_ref[h] = jnp.broadcast_to(columns[:, h : h + 1], (width, LANES))


def decay_blocks(cs_row, column):
    count = cs_row.shape[1] // LANES
    out = {}
    for i in range(count):
        for j in range(i, count):
            gap = cs_row[:, j * LANES : (j + 1) * LANES] - column[i * LANES : (i + 1) * LANES]
            out[i, j] = jnp.exp2(jnp.minimum(gap, 0.0) if i == j else gap)
    return out


def block(ref, i, j):
    return ref[i * LANES : (i + 1) * LANES, j * LANES : (j + 1) * LANES]


def mixing(decay, score_ref):
    count = score_ref.shape[0] // LANES
    none = jnp.zeros((LANES, LANES), BF)
    return jnp.concatenate(
        [
            jnp.concatenate(
                [
                    (decay[i, j] * block(score_ref, i, j)).astype(BF) if j >= i else none
                    for j in range(count)
                ],
                1,
            )
            for i in range(count)
        ],
        0,
    )


def loop_heads(heads, compute, store):
    group = GROUP if heads % GROUP == 0 else 1

    def some(i, carry):
        done = [compute(i * group + u) for u in range(group)]
        store(done)
        return carry

    lax.fori_loop(0, heads // group, some, 0)


def forward_kernel(
    heads, me, raw, bc_raw, dt_raw, cw, cbw, hp,
    z_out, y_out, cs_out, mem_out, zbc_out,
    mem, before, before_bc, step_s, cs_s, col_s, ecs_s, rem_s, end_s, score_s, maps_s,
):
    head_size = raw.shape[2] // heads
    half = bc_raw.shape[2] // 2
    width = raw.shape[3]
    taps = cw.shape[0]

    @pl.when(pl.program_id(1) == 0)
    def _():
        mem[...] = jnp.zeros_like(mem)
        before[...] = jnp.zeros_like(before)
        before_bc[...] = jnp.zeros_like(before_bc)

    bc = bc_raw[0, 0].astype(F32)
    zbc = conv_rows(bc, before_bc[...], [cbw[j] for j in range(taps)])
    before_bc[...] = bc[:, width - LANES :]
    zbc_out[0, 0] = zbc
    maps_s[...] = (zbc * jax.nn.sigmoid(zbc)).astype(BF)
    causal = order_mask(width, lambda s, t: s <= t)
    score_s[...] = jnp.where(causal, dot(maps_s[:half], maps_s[half:], TN), 0.0)

    _, step, a_decay = head_rows(dt_raw[0, 0], hp[0], hp[1])
    cs = jnp.dot(step * a_decay, causal.astype(F32), precision=HIGH, preferred_element_type=F32)
    cs_out[0, 0] = cs
    step_s[...] = step
    fill_heads(cs, heads, cs_s, col_s, ecs_s, rem_s, end_s)

    def compute(h):
        rows = pl.ds(pl.multiple_of(h * head_size, head_size), head_size)
        row = pl.ds(h, 1)
        own = raw[0, 0, rows, :].astype(F32)
        z = conv_rows(own, before[rows, :], [cw[j, rows, :] for j in range(taps)])
        x = z * jax.nn.sigmoid(z)
        scaled = x * step_s[row, :]
        decay = decay_blocks(cs_s[row, :], col_s[h])
        inside = dot(scaled.astype(BF), mixing(decay, score_s), NN)
        memory = mem[rows, :]
        memory_low = memory.astype(BF)
        held = dot(memory_low, maps_s[half:], NN) * ecs_s[row, :]
        y = inside + held + hp[2, row, :] * x
        gained = dot((scaled * rem_s[row, :]).astype(BF), maps_s[:half], NT)
        return rows, own[:, width - LANES :], z, y, memory_low, memory * end_s[row, :] + gained

    def store(done):
        for rows, edge, z, y, memory_low, memory in done:
            before[rows, :] = edge
            z_out[0, 0, rows, :] = z
            y_out[0, 0, rows, :] = y
            mem_out[0, 0, rows, :] = memory_low
            mem[rows, :] = memory

    loop_heads(heads, compute, store)


def backward_kernel(
    heads, me, z_in, raw, y_in, g_in, zbc_in, bc_raw, dt_raw, cs_in, mem_in, cw, cbw, hp,
    grad_out, sum_x, sum_bc, sum_h,
    gmem, gmem_low, after, after_bc, step_s, cs_s, col_s, ecs_s, rem_s, end_s, score_s, maps_s,
    gscore_s, eg_s, rx_s, pq_s, e_s, r_s, d_s, k_s,
):
    inner = raw.shape[2]
    head_size = inner // heads
    half = zbc_in.shape[2] // 2
    width = raw.shape[3]
    taps = cw.shape[0]

    @pl.when((pl.program_id(0) == 0) & (pl.program_id(1) == 0))
    def _():
        sum_x[...] = jnp.zeros_like(sum_x)
        sum_h[...] = jnp.zeros_like(sum_h)
        pq_s[...] = jnp.zeros_like(pq_s)
        e_s[...] = jnp.zeros_like(e_s)
        r_s[...] = jnp.zeros_like(r_s)
        d_s[...] = jnp.zeros_like(d_s)
        k_s[...] = jnp.zeros_like(k_s)
        sum_bc[...] = jnp.zeros_like(sum_bc)

    @pl.when(pl.program_id(1) == 0)
    def _():
        gmem[...] = jnp.zeros_like(gmem)
        after[...] = jnp.zeros_like(after)
        after_bc[...] = jnp.zeros_like(after_bc)

    zbc = zbc_in[0, 0]
    sig_bc = jax.nn.sigmoid(zbc)
    maps_s[...] = (zbc * sig_bc).astype(BF)
    causal = order_mask(width, lambda s, t: s <= t)
    score_s[...] = jnp.where(causal, dot(maps_s[:half], maps_s[half:], TN), 0.0)
    gscore_s[...] = jnp.zeros_like(gscore_s)

    biased, step, a_decay = head_rows(dt_raw[0, 0], hp[0], hp[1])
    step_s[...] = step
    fill_heads(cs_in[0, 0], heads, cs_s, col_s, ecs_s, rem_s, end_s)

    def compute(h):
        rows = pl.ds(pl.multiple_of(h * head_size, head_size), head_size)
        row = pl.ds(h, 1)
        z = z_in[0, 0, rows, :]
        sig = jax.nn.sigmoid(z)
        x = z * sig
        step_row = step_s[row, :]
        skip = hp[2, row, :]
        scaled = x * step_row
        scaled_low = scaled.astype(BF)
        scaled_back = scaled_low.astype(F32)
        g_low = g_in[0, 0, rows, :]
        g = g_low.astype(F32)
        decay = decay_blocks(cs_s[row, :], col_s[h])
        inside = dot(g_low, mixing(decay, score_s), NT)
        gweights = dot(scaled_low, g_low, TN)
        gscore = {
            (i, j): weight * gweights[i * LANES : (i + 1) * LANES, j * LANES : (j + 1) * LANES]
            for (i, j), weight in decay.items()
        }
        later = gmem[rows, :]
        later_low = later.astype(BF)
        outside = dot(later_low, maps_s[:half], NN) * rem_s[row, :]
        gscaled = inside + outside
        both = g * (y_in[0, 0, rows, :] - skip * x) - scaled_back * inside
        sums = (
            jnp.sum(both, 0, keepdims=True),
            jnp.sum(scaled_back * outside, 0, keepdims=True),
            jnp.sum(x * gscaled, 0, keepdims=True),
            d_s[row, :] + jnp.sum(g * x, 0, keepdims=True),
            jnp.sum(later * mem_in[0, 0, rows, :].astype(F32), 0, keepdims=True),
        )
        eg = (g * ecs_s[row, :]).astype(BF)
        rx = (scaled * rem_s[row, :]).astype(BF)
        earlier = later * end_s[row, :] + dot(eg, maps_s[half:], NT)
        gz = (step_row * gscaled + skip * g) * (sig * (1.0 + z * (1.0 - sig)))
        grad, terms = conv_back(
            gz, after[rows, :], raw[0, 0, rows, :].astype(F32),
            [cw[j, rows, :] for j in range(taps)],
        )
        terms = [sum_x[j, rows, :] + term for j, term in enumerate(terms)]
        return rows, row, gscore, sums, later_low, eg, rx, earlier, gz[:, :LANES], grad, terms

    def store(done):
        for i, j in done[0][2]:
            place = (slice(i * LANES, (i + 1) * LANES), slice(j * LANES, (j + 1) * LANES))
            gscore_s[place] += sum(one[2][i, j] for one in done)
        for rows, row, _, sums, later_low, eg, rx, earlier, edge, grad, terms in done:
            for ref, value in zip((pq_s, e_s, r_s, d_s, k_s), sums):
                ref[row, :] = value
            gmem_low[rows, :] = later_low
            eg_s[rows, :] = eg
            rx_s[rows, :] = rx
            gmem[rows, :] = earlier
            after[rows, :] = edge
            grad_out[0, 0, rows, :] = grad.astype(BF)
            for j, term in enumerate(terms):
                sum_x[j, rows, :] = term

    loop_heads(heads, compute, store)

    gscore = jnp.where(causal, gscore_s[...], 0.0).astype(BF)
    gout_map = dot(maps_s[:half], gscore, NN) + dot(mem_in[0, 0], eg_s[...], TN)
    gin_map = dot(maps_s[half:], gscore, NT) + dot(gmem_low[...], rx_s[...], TN)
    gmaps = jnp.concatenate([gin_map, gout_map], 0) * (sig_bc * (1.0 + zbc * (1.0 - sig_bc)))
    gbc, terms = conv_back(
        gmaps, after_bc[...], bc_raw[0, 0].astype(F32), [cbw[j] for j in range(taps)]
    )
    for j, term in enumerate(terms):
        sum_bc[j] += term
    after_bc[...] = gmaps[:, :LANES]
    grad_out[0, 0, inner : inner + 2 * half, :] = gbc.astype(BF)

    from_here = order_mask(width, lambda t, u: t >= u).astype(F32)
    strictly = order_mask(width, lambda s, u: s < u).astype(F32)
    carried = jnp.sum(k_s[...], 1, keepdims=True) * end_s[:, :1]
    gdecay = (
        jnp.dot(pq_s[...], from_here, precision=HIGH, preferred_element_type=F32)
        + jnp.dot(e_s[...], strictly, precision=HIGH, preferred_element_type=F32)
        + carried
    )
    gdt = (a_decay * gdecay + r_s[...]) * jax.nn.sigmoid(biased)
    grad_out[0, 0, inner + 2 * half :, :] = gdt.astype(BF)
    sum_h[0] += fold(gdt)
    sum_h[1] += fold(gdecay * step * a_decay)

    @pl.when((pl.program_id(0) == pl.num_programs(0) - 1) & (pl.program_id(1) == pl.num_programs(1) - 1))
    def _():
        sum_h[2] = fold(d_s[...])


def head_scratch(head_pad, heads, width, maps):
    return [
        pltpu.VMEM((head_pad, width), F32),
        pltpu.VMEM((head_pad, width), F32),
        pltpu.VMEM((heads, width, LANES), F32),
        pltpu.VMEM((head_pad, width), F32),
        pltpu.VMEM((head_pad, width), F32),
        pltpu.VMEM((head_pad, LANES), F32),
        pltpu.VMEM((width, width), F32),
        pltpu.VMEM((maps, width), BF),
    ]


def fixed(array):
    return pl.BlockSpec(array.shape, lambda s, c, me: (0,) * len(array.shape))


def kernel_call(body, name, flops, reverse, inputs, kinds, outs, scratch):
    parts, seqs = inputs[0].shape[:2]

    def part(array):
        def place(s, c, me):
            return ((parts - 1 - c if reverse else c) ^ me[0], s, 0, 0)

        return pl.BlockSpec((1, 1) + array.shape[2:], place)

    def spec(array, kind):
        return part(array) if kind == "p" else fixed(array)

    return pl.pallas_call(
        body,
        grid_spec=pltpu.PrefetchScalarGridSpec(
            num_scalar_prefetch=1,
            grid=(seqs, parts),
            in_specs=[spec(x, k) for x, k in zip(inputs, kinds)],
            out_specs=[spec(x, k) for x, k in outs],
            scratch_shapes=scratch,
        ),
        out_shape=[x for x, _ in outs],
        compiler_params=pltpu.CompilerParams(
            dimension_semantics=("arbitrary", "arbitrary"), vmem_limit_bytes=48 << 20
        ),
        cost_estimate=pl.CostEstimate(flops=flops, bytes_accessed=16 << 20, transcendentals=0),
        name=name,
    )(lax.axis_index("ctx").reshape(1), *inputs)


def run_forward(inner, bc, dt, cw, cbw, hp, heads):
    parts, seqs, rows, width = inner.shape
    maps, head_pad, states = bc.shape[2], dt.shape[2], bc.shape[2] // 2

    def out(count, last=width, kind=F32):
        return jax.ShapeDtypeStruct((parts, seqs, count, last), kind), "p"

    scratch = [
        pltpu.VMEM((rows, states), F32), pltpu.VMEM((rows, LANES), F32), pltpu.VMEM((maps, LANES), F32),
    ]
    return kernel_call(
        partial(forward_kernel, heads), "scan_forward", 45 << 30, False,
        [inner, bc, dt, cw, cbw, hp], "pppfff",
        [out(rows), out(rows), out(head_pad), out(rows, states, BF), out(maps)],
        scratch + head_scratch(head_pad, heads, width, maps),
    )


def run_backward(z, inner, y, g, zbc, bc, dt, cs, mem, cw, cbw, hp, heads):
    parts, seqs, rows, width = inner.shape
    maps, head_pad, states = zbc.shape[2], dt.shape[2], zbc.shape[2] // 2
    grads = jax.ShapeDtypeStruct((parts, seqs, rows + maps + head_pad, width), BF)
    sums = [cw.shape, cbw.shape, (3, head_pad, LANES)]
    scratch = [
        pltpu.VMEM((rows, states), F32), pltpu.VMEM((rows, states), BF),
        pltpu.VMEM((rows, LANES), F32), pltpu.VMEM((maps, LANES), F32),
    ]
    scratch += head_scratch(head_pad, heads, width, maps)
    scratch += [
        pltpu.VMEM((width, width), F32), pltpu.VMEM((rows, width), BF), pltpu.VMEM((rows, width), BF),
    ]
    scratch += [pltpu.VMEM((head_pad, width), F32)] * 4 + [pltpu.VMEM((head_pad, LANES), F32)]
    return kernel_call(
        partial(backward_kernel, heads), "scan_backward", 60 << 30, True,
        [z, inner, y, g, zbc, bc, dt, cs, mem, cw, cbw, hp], "pppppppppfff",
        [(grads, "p")] + [(jax.ShapeDtypeStruct(x, F32), "f") for x in sums], scratch,
    )


def project(rows, weight):
    return jnp.einsum("ksld,di->ksil", rows, weight, preferred_element_type=F32)


def project_back(grad, weight):
    return jnp.einsum("ksil,di->ksld", grad, weight, preferred_element_type=F32)


def weight_grad(rows, grad):
    return jnp.einsum("ksld,ksil->di", rows, grad, preferred_element_type=F32)


def per_device(
    tokens, norm_gain, w_zx, w_dt, w_bc, conv_x_w, conv_x_b, conv_bc_w, conv_bc_b,
    dt_bias, a_log, d_skip, norm_w, w_out, output_gradient,
):
    seqs_here, length, width = tokens.shape
    heads = w_dt.shape[1]
    head_pad = -(-heads // 16) * 16
    inner_here = w_out.shape[1]
    inner_total = inner_here * lax.axis_size("tensor")
    maps = w_bc.shape[1]
    rest = inner_here + maps
    dp_bits = [("dp", b) for b in bits_of("dp")]
    ctx_bits = [("ctx", b) for b in bits_of("ctx")]
    ways = [ctx_bits, ctx_bits[::-1]]
    tensor_bits = [("tensor", b) for b in bits_of("tensor")]

    def lanes(column):
        return jnp.broadcast_to(column[..., None], column.shape + (LANES,))

    cw = lanes(jnp.concatenate([conv_x_w, conv_x_b[None]], 0))
    cbw = lanes(jnp.concatenate([conv_bc_w, conv_bc_b[None]], 0))
    hp = jnp.pad(jnp.stack([dt_bias, a_log, d_skip]), ((0, 0), (0, head_pad - heads)))
    hp = jnp.broadcast_to(hp[..., None], hp.shape + (length,))

    rows = spread_out(tokens, length)
    scan_weights = jnp.concatenate(
        [w_zx[:, 1], w_bc, jnp.pad(w_dt, ((0, 0), (0, head_pad - heads)))], 1
    )
    cut = inner_here // 2 + LANES
    scan_weights = both_ways(scan_weights, cut)
    scan_weights[0] = jnp.concatenate([scan_weights[0], norm_gain[:, None]], 1)
    scan_weights = [open_gather(x) for x in scan_weights]
    for place in dp_bits:
        scan_weights = [double(x, place) for x in scan_weights]
    outer = jnp.concatenate([w_out, w_zx[:, 0]], 1)
    rows, scan_weights, outer, cw, cbw, hp = tie(rows, scan_weights, outer, cw, cbw, hp)
    outer = lax.all_gather(outer, ("dp", "ctx"), axis=0, tiled=True)
    for places in zip(*ways):
        scan_weights = [double(x, place) for x, place in zip(scan_weights, places)]
    first, second = [close_gather(x) for x in scan_weights]
    full_scan = jnp.concatenate([first[:, :cut], second], 1)
    gain = first[:, cut].astype(F32)
    rows = gather_cuts(jnp.stack(rows))
    rows, cot_ready = tie(rows, output_gradient)
    cots = spread_out(cot_ready, length)

    residual = rows.astype(F32)
    normed = (
        residual * lax.rsqrt(jnp.mean(residual * residual, axis=-1, keepdims=True) + EPS) * gain
    ).astype(BF)
    inner_raw = project(normed, full_scan[:, :inner_here]).astype(BF)
    bc_raw = project(normed, full_scan[:, inner_here:rest]).astype(BF)
    dt_raw = project(normed, full_scan[:, rest:])
    z, y, cs, mem, zbc = run_forward(inner_raw, bc_raw, dt_raw, cw, cbw, hp, heads)

    y, outer, cots = tie(y, outer, cots)
    cots = gather_cuts(jnp.stack(cots))
    full_out, full_gate = outer[:, :inner_here], outer[:, inner_here:]
    norm_column = norm_w[:, None]
    gate_raw = project(normed, full_gate)
    grad_mixed = project(cots, full_out)
    gate_sig = jax.nn.sigmoid(gate_raw)
    gate_act = gate_raw * gate_sig
    gated = y * gate_act
    weighted = grad_mixed * norm_column
    sums = jnp.stack([jnp.sum(gated * gated, axis=2), jnp.sum(weighted * gated, axis=2)])
    sums = sum_over(sums, tensor_bits)[:, :, :, None]
    inv_rms = lax.rsqrt(sums[0] / inner_total + EPS)
    mixed_in = (gated * inv_rms * norm_column).astype(BF)
    grad_norm_w = jnp.sum(grad_mixed * gated * inv_rms, axis=(0, 1, 3))
    grad_gated = inv_rms * weighted - gated * (inv_rms * inv_rms * inv_rms) * (
        sums[1] / inner_total
    )
    grad_gate = (grad_gated * y * gate_sig * (1.0 + gate_raw * (1.0 - gate_sig))).astype(BF)
    grad_y = (grad_gated * gate_act).astype(BF)

    outer_grad = jnp.concatenate(
        [weight_grad(cots, mixed_in).astype(BF), weight_grad(normed, grad_gate).astype(BF)], 1
    )
    mixed_in, grad_gate, outer_grad = tie(mixed_in, grad_gate, outer_grad)
    outer_grad = offer(open_scatter(outer_grad), 1, "ctx")
    cuts = lax.axis_size("tensor")
    share = lax.dynamic_slice_in_dim(
        rows, lax.axis_index("tensor") * (length // cuts), length // cuts, 2
    ).astype(F32)
    mixed = (share + own_share(shares(mixed_in, full_out))).astype(BF)
    normed_gate = [x.astype(BF) for x in shares(grad_gate, full_gate)]
    grad_y, mixed, normed_gate = tie(grad_y, mixed, normed_gate)
    mixed = send_home(mixed)

    grad_scan, sum_x, sum_bc, sum_h = run_backward(
        z, inner_raw, y, grad_y, zbc, bc_raw, dt_raw, cs, mem, cw, cbw, hp, heads
    )
    grad_scan, sum_x, sum_bc, sum_h, mixed, outer_grad = tie(
        grad_scan, sum_x, sum_bc, sum_h, mixed, outer_grad
    )

    sum_x = jnp.sum(sum_x, -1)
    sum_bc = jnp.sum(sum_bc, -1)
    sum_h = jnp.sum(sum_h, -1)[:, :heads]
    pieces = [sum_x, grad_norm_w, sum_h, sum_bc]
    flat = jnp.concatenate([p.reshape(-1) for p in pieces])
    size = flat.shape[0]
    flat = jnp.pad(flat, (0, -size % 1024)).reshape(-1, LANES)
    flat = sum_over(flat, ctx_bits + dp_bits).reshape(-1)[:size]
    out = []
    for p in pieces:
        out.append(flat[: p.size].reshape(p.shape))
        flat = flat[p.size :]
    sum_x, grad_norm_w, sum_h, sum_bc = out
    sum_bc = sum_over(sum_bc, tensor_bits)
    taps = conv_x_w.shape[0]

    scan_grad = weight_grad(normed, grad_scan).astype(BF)
    grad_scan, scan_grad = tie(grad_scan, scan_grad)
    scan_grad = offer(open_scatter(scan_grad), 1, "ctx")
    outer_grad = scatter_dp(add_up(outer_grad))
    grad_share = [
        x.astype(F32) + part for x, part in zip(normed_gate, shares(grad_scan, full_scan))
    ]
    grad_share = own_share(grad_share).astype(BF)
    grad_share, scan_grad = tie(grad_share, scan_grad)
    grad_home = send_home(grad_share)
    scan_grad = scatter_dp(add_up(scan_grad))
    grad_w_out, grad_w_gate = outer_grad[:, :inner_here], outer_grad[:, inner_here:]
    grad_w_inner = scan_grad[:, :inner_here]
    grad_w_bc = sum_over(scan_grad[:, inner_here:rest], tensor_bits)
    grad_w_dt = scan_grad[:, rest : rest + heads]
    r = lax.rsqrt(jnp.mean(share * share, axis=-1, keepdims=True) + EPS)
    grad_gain = jnp.sum(share * r * grad_share.astype(F32), axis=(0, 1, 2))

    grad_gain = sum_over(grad_gain.reshape(-1, LANES), tensor_bits + dp_bits + ctx_bits).reshape(-1)
    row = lax.axis_index("dp") * lax.axis_size("ctx") + lax.axis_index("ctx")
    grad_gain = lax.dynamic_slice_in_dim(
        grad_gain, row * norm_gain.shape[0], norm_gain.shape[0], 0
    )

    mixed_out = arrange(mixed)
    grad_home = arrange(grad_home).astype(F32)
    here = tokens.astype(F32)
    r = lax.rsqrt(jnp.mean(here * here, axis=-1, keepdims=True) + EPS)
    scaled = gain * grad_home
    grad_tokens = (
        output_gradient.astype(F32)
        + r * scaled
        - here * (r * r * r) * jnp.mean(here * scaled, axis=-1, keepdims=True)
    )
    return (
        mixed_out,
        grad_tokens,
        grad_gain,
        jnp.stack([grad_w_gate, grad_w_inner], 1),
        grad_w_dt,
        grad_w_bc,
        sum_x[:taps],
        sum_x[taps],
        sum_bc[:taps],
        sum_bc[taps],
        sum_h[0],
        sum_h[1],
        sum_h[2],
        grad_norm_w,
        grad_w_out,
    )


def solution(mesh):
    rows = P(("dp", "ctx"), "tensor")
    tokens = P("dp", "ctx", None)
    heads = P("tensor")
    return jax.shard_map(
        per_device,
        mesh=mesh,
        in_specs=(
            tokens, P(("dp", "ctx")), P(("dp", "ctx"), None, "tensor"), rows, P(("dp", "ctx"), None),
            P(None, "tensor"), heads, P(), P(), heads, heads, heads, heads, rows, tokens,
        ),
        out_specs=(
            tokens, tokens, P(("dp", "ctx")), P(("dp", "ctx"), None, "tensor"), rows,
            P(("dp", "ctx"), None), P(None, "tensor"), heads, P(), P(), heads, heads, heads, heads, rows,
        ),
        check_vma=False,
    )
```
